512 devices in a mesh: gy: 32 (over y, x, core), gz: 16 (over z).
Axes of the slice: x: 4, y: 4, z: 16, core: 2. Of those that a mesh axis runs over, the one named last changes fastest.
Arguments:
- fluid_state: float32 [5, 8, 2048, 2048], P(None, None, 'gy', 'gz'), may hold values from -1 to 3, as said below
- tracer_cell: int32 [32, 16, 16, 128], P('gy', 'gz'), may hold values from 0 to 4095
- tracer_owner: int32 [32, 16, 16], P('gy', 'gz'), may hold values from 0 to 15, as said below
- tracer_count: int32 [32, 16, 16], P('gy', 'gz'), may hold values from 32 to 128, as said below
- tracer_peak: float32 [32, 16, 16, 128], P('gy', 'gz'), may hold values from 0.5 to 2.5
Outputs:
- new_state: float32 [5, 8, 2048, 2048], P(None, None, ('gy', 'gz'))
- new_peak: float32 [32, 16, 16, 128], P('gy', 'gz')
The draws below stay inside these ranges and needn't reach their ends.
Inputs may be any that keep to these rules, and one draw needn't show every extreme that they name: `fluid_state`: density from 0.5 to 3, velocities from -1 to 1, pressure from 0.5 to 2.5. `tracer_owner`: the blocks held at one index of gy and gz name every owner once. `tracer_count`: each count is 128 or lies between 32 and 64; at each index of gy one owner gets a full block from every index of gz.
All inputs are finite; a program needn't handle non-finite values.
Results may differ from the reference program's by a relative error of at most 0.000075.
Values sent between devices are 32-bit elements; how exact they have to be, the bound alone decides.
No kernel may reach another device: no remote copies, remote signals or barrier semaphores. Data moves between devices by JAX's collectives and lax.ppermute only.
A program may use at most 128 MiB of HBM per device.

```python
import jax
import jax.numpy as jnp
from jax import lax

NX = 8
CY = 64
CZ = 128
CAP = 128
NY = 2048
NZ = 2048
SUB = 4
N_GY = 32
N_GZ = 16


def owner_table(key):
    subkeys = jax.random.split(key, N_GY * N_GZ)
    orders = jax.vmap(lambda one_key: jax.random.permutation(one_key, N_GZ))(subkeys)
    return orders.reshape(N_GY, N_GZ, N_GZ).astype(jnp.int32)


def draw_tracer_owner(key, part):
    table = owner_table(key)
    return table


def draw_tracer_count(key, part):
    table = owner_table(key)
    key = jax.random.fold_in(key, 7)
    hottest = jax.random.randint(jax.random.fold_in(key, 1), (N_GY, 1, 1), 0, N_GZ)
    drawn = jax.random.randint(jax.random.fold_in(key, 2), (N_GY, N_GZ, N_GZ), CAP // 4, CAP // 2 + 1)
    return jnp.where(table == hottest, CAP, drawn).astype(jnp.int32)


def draw_fluid_state(key, part):
    key = jax.random.fold_in(key, 11)
    rough_u = jax.random.uniform(key, (5, NX, NY, NZ), jnp.float32)
    mixed = rough_u
    density = 0.5 * jnp.power(6.0, mixed[0])
    velocity = 2.0 * mixed[1:4] - 1.0
    pressure = 0.5 * jnp.power(5.0, mixed[4])
    return jnp.concatenate([density[None], velocity, pressure[None]], axis=0).astype(jnp.float32)


def plant(entries, rng, low, high):
    shape = entries.shape
    place = [jax.random.randint(jax.random.fold_in(rng, axis), (), 0, shape[axis]) for axis in range(len(shape))]
    entries = entries.at[tuple(place)].set(low)
    longest = shape.index(max(shape))
    place[longest] = (place[longest] + 1) % shape[longest]
    return entries.at[tuple(place)].set(high)


def steps_of(stream_key, shape, cuts, low, high):
    def one(dim, blocks):
        draws = jax.random.uniform(jax.random.fold_in(jax.random.fold_in(stream_key, 6), dim), (blocks,), jnp.float32, low / len(cuts), high / len(cuts))
        return jnp.repeat(jnp.exp(draws), shape[dim] // blocks).reshape((-1,) + (1,) * (len(shape) - dim - 1))

    gain = one(*cuts[0])
    for cut in cuts[1:]:
        gain = gain * one(*cut)
    return gain


def setup_inputs(seed: int = 0) -> dict:
    key_list = jax.random.split(jax.random.key(seed), 6)
    return {
        "fluid_state": draw_fluid_state(jax.random.fold_in(key_list[5], 71), 0),
        "tracer_cell": plant(jax.random.randint(key_list[1], (N_GY, N_GZ, N_GZ, CAP), 0, NX * SUB * CZ), jax.random.fold_in(key_list[1], 1), 0, (NX * SUB * CZ) - 1).astype(jnp.int32),
        "tracer_owner": draw_tracer_owner(jax.random.fold_in(key_list[5], 71), 0),
        "tracer_count": draw_tracer_count(jax.random.fold_in(key_list[5], 71), 0),
        "tracer_peak": jnp.clip(0.5 + 2.0 * jax.random.uniform(key_list[4], (N_GY, N_GZ, N_GZ, CAP), jnp.float32) ** steps_of(key_list[4], (N_GY, N_GZ, N_GZ, CAP), ((0, 32), (1, 16)), -0.2, 0.2), 0.5, 2.5),
    }


GAMMA = 1.4
RATIO = 0.06

def median_of(first, second, third):
    return jnp.maximum(jnp.minimum(first, second), jnp.minimum(jnp.maximum(first, second), third))

def slice_of(values, offset, length, along):
    return lax.slice_in_dim(values, offset, offset + length, axis=along)

def conserved(fields):
    density = fields[0]
    kinetic = 0.5 * density * (fields[1] * fields[1] + fields[2] * fields[2] + fields[3] * fields[3])
    return jnp.stack([density, density * fields[1], density * fields[2], density * fields[3], fields[4] / (GAMMA - 1.0) + kinetic])

def primitive(totals):
    density = totals[0]
    vel_x = totals[1] / density
    vel_y = totals[2] / density
    vel_z = totals[3] / density
    kinetic = 0.5 * (totals[1] * vel_x + totals[2] * vel_y + totals[3] * vel_z)
    return jnp.stack([density, vel_x, vel_y, vel_z, (GAMMA - 1.0) * (totals[4] - kinetic)])

def physical_flux(fields, totals, normal):
    normal_vel = fields[normal]
    pieces = [totals[k] * normal_vel for k in range(5)]
    pieces[normal] = pieces[normal] + fields[4]
    pieces[4] = (totals[4] + fields[4]) * normal_vel
    return jnp.stack(pieces)

def advance(extended, along, normal):
    interior_n = extended.shape[along] - 6
    faces_n = interior_n + 3
    face_val = 7.0 / 12.0 * (slice_of(extended, 1, faces_n, along) + slice_of(extended, 2, faces_n, along)) - 1.0 / 12.0 * (slice_of(extended, 0, faces_n, along) + slice_of(extended, 3, faces_n, along))
    lower_bound = jnp.minimum(slice_of(extended, 1, faces_n, along), slice_of(extended, 2, faces_n, along))
    upper_bound = jnp.maximum(slice_of(extended, 1, faces_n, along), slice_of(extended, 2, faces_n, along))
    face_val = jnp.minimum(jnp.maximum(face_val, lower_bound), upper_bound)
    centre = slice_of(extended, 2, interior_n + 2, along)
    left_gap = centre - slice_of(face_val, 0, interior_n + 2, along)
    right_gap = slice_of(face_val, 1, interior_n + 2, along) - centre
    edge_left = centre - median_of(0.0, left_gap, 2.0 * right_gap)
    edge_right = centre + median_of(0.0, right_gap, 2.0 * left_gap)
    state_left = slice_of(edge_right, 0, interior_n + 1, along)
    state_right = slice_of(edge_left, 1, interior_n + 1, along)
    totals_left = conserved(state_left)
    totals_right = conserved(state_right)
    sound_left = jnp.sqrt(GAMMA * state_left[4] / state_left[0])
    sound_right = jnp.sqrt(GAMMA * state_right[4] / state_right[0])
    slowest = jnp.minimum(jnp.minimum(state_left[normal] - sound_left, state_right[normal] - sound_right), 0.0)
    fastest = jnp.maximum(jnp.maximum(state_left[normal] + sound_left, state_right[normal] + sound_right), 0.0)
    flux_left = physical_flux(state_left, totals_left, normal)
    flux_right = physical_flux(state_right, totals_right, normal)
    face_flux = (fastest * flux_left - slowest * flux_right + slowest * fastest * (totals_right - totals_left)) / (fastest - slowest)
    interior = conserved(slice_of(extended, 3, interior_n, along))
    updated = interior - RATIO * (slice_of(face_flux, 1, interior_n, along) - slice_of(face_flux, 0, interior_n, along))
    return primitive(updated)

def wrap_pad(fields, along):
    length = fields.shape[along]
    return jnp.concatenate([slice_of(fields, length - 3, 3, along), fields, slice_of(fields, 0, 3, along)], axis=along)

def reference(fluid_state, tracer_cell, tracer_owner, tracer_count, tracer_peak):

    def slab_plane(plane_fields):
        middle = advance(wrap_pad(plane_fields, 1), 1, 2)
        return advance(wrap_pad(middle, 2), 2, 3)
    planes = lax.map(slab_plane, jnp.moveaxis(fluid_state, 1, 0))
    new_state = jnp.moveaxis(planes, 0, 1)
    pressure = new_state[4]
    grid_y = lax.broadcasted_iota(jnp.int32, tracer_cell.shape, 0)
    grid_z = lax.broadcasted_iota(jnp.int32, tracer_cell.shape, 1)
    slot_idx = lax.broadcasted_iota(jnp.int32, tracer_cell.shape, 3)
    owners_row = tracer_owner[:, :, :, None]
    plane_ids = tracer_cell // (SUB * CZ)
    row_ids = grid_y * CY + owners_row * SUB + tracer_cell // CZ % SUB
    col_ids = grid_z * CZ + tracer_cell % CZ
    sampled = pressure[plane_ids, row_ids, col_ids]
    live_mask = slot_idx < tracer_count[:, :, :, None]
    new_peak = jnp.where(live_mask, jnp.maximum(tracer_peak, sampled), jnp.zeros_like(tracer_peak))
    return (new_state, new_peak)
```

```python
import jax
import jax.numpy as jnp
from jax import lax
from jax.experimental import pallas as pl
from jax.experimental.pallas import tpu as pltpu
from jax.sharding import PartitionSpec as P

GAMMA = 1.4
RATIO = 0.06
LANES = 128


def median_of(first, second, third):
    return jnp.maximum(jnp.minimum(first, second), jnp.minimum(jnp.maximum(first, second), third))


def face_of(before, left, right, after):
    out = []
    for b, l, r, a in zip(before, left, right, after):
        mid = (7.0 / 12.0) * (l + r) - (1.0 / 12.0) * (b + a)
        out.append(jnp.minimum(jnp.maximum(mid, jnp.minimum(l, r)), jnp.maximum(l, r)))
    return out


def edges_of(centre, face_left, face_right):
    left, right = [], []
    for a, fl, fr in zip(centre, face_left, face_right):
        triple = 3.0 * a
        left.append(median_of(a, fl, triple - 2.0 * fr))
        right.append(median_of(a, fr, triple - 2.0 * fl))
    return left, right


def inverse(value):
    guess = pl.reciprocal(value, approx=True)
    return guess * (2.0 - value * guess)


def flux_of(left, right, normal):
    rho_l, p_l, u_l = left[0], left[4], left[normal]
    rho_r, p_r, u_r = right[0], right[4], right[normal]
    c_l = jnp.sqrt(GAMMA * p_l * inverse(rho_l))
    c_r = jnp.sqrt(GAMMA * p_r * inverse(rho_r))
    slow = jnp.minimum(jnp.minimum(u_l - c_l, u_r - c_r), 0.0)
    fast = jnp.maximum(jnp.maximum(u_l + c_l, u_r + c_r), 0.0)
    scale = RATIO * inverse(fast - slow)
    a_l = fast * scale
    a_r = -slow * scale
    w_l = a_l * (u_l - slow)
    w_r = a_r * (u_r - fast)
    q_l = rho_l * w_l
    q_r = rho_r * w_r
    flux = [q_l + q_r] + [q_l * left[k] + q_r * right[k] for k in (1, 2, 3)]
    flux[normal] = flux[normal] + (a_l * p_l + a_r * p_r)
    square_l = left[1] * left[1] + left[2] * left[2] + left[3] * left[3]
    square_r = right[1] * right[1] + right[2] * right[2] + right[3] * right[3]
    heat = p_l * (2.5 * w_l + a_l * u_l) + p_r * (2.5 * w_r + a_r * u_r)
    flux.append(0.5 * (q_l * square_l + q_r * square_r) + heat)
    return flux


def updated(state, flux_left, flux_right):
    rho, vx, vy, vz, p = state
    mom = [rho * v for v in (vx, vy, vz)]
    energy = 2.5 * p + 0.5 * (mom[0] * vx + mom[1] * vy + mom[2] * vz)
    totals = [
        t - (r - l) for t, l, r in zip([rho] + mom + [energy], flux_left, flux_right)
    ]
    inv = inverse(totals[0])
    vel = [totals[k] * inv for k in (1, 2, 3)]
    kinetic = 0.5 * (totals[1] * vel[0] + totals[2] * vel[1] + totals[3] * vel[2])
    return [totals[0]] + vel + [0.4 * (totals[4] - kinetic)]


def lane_after(here, following, lane):
    return [
        pltpu.roll(jnp.where(lane == 0, f, h), LANES - 1, 1) for h, f in zip(here, following)
    ]


def lane_before(here, previous, lane):
    return [
        pltpu.roll(jnp.where(lane == LANES - 1, p, h), 1, 1) for h, p in zip(here, previous)
    ]


def sweep_y_kernel(fluid_ref, low_ref, high_ref, middle_ref, edge_ref):
    rows_y = fluid_ref.shape[1] // 8
    blocks = middle_ref.shape[0]
    lane = lax.broadcasted_iota(jnp.int32, (8, LANES), 1)

    def row(y):
        return [fluid_ref[k, pl.ds(y, 8, stride=rows_y), :] for k in range(5)]

    def low(i):
        return [low_ref[i, k] for k in range(5)]

    def high(i):
        return [high_ref[i, k] for k in range(5)]

    def block(h, carry, load, packed):
        flux, right, face, c0, c1, c2 = carry
        first, second = packed
        for sub in range(4):
            c3 = load(sub)
            face_next = face_of(c0, c1, c2, c3)
            left_next, right_next = edges_of(c1, face, face_next)
            flux_next = flux_of(right, left_next, 2)
            new = updated(c0, flux, flux_next)
            spot = 4 * (h * 4 + sub) % LANES
            group = lane // 4 == spot // 4
            for k in range(5):
                middle_ref[h, k, pl.ds(sub, 8, stride=4), :] = new[k]
            first = [
                jnp.where(group, pltpu.roll(v, spot, 1), f) for v, f in zip(new, first)
            ]
            second = [
                jnp.where(group, pltpu.roll(v, (spot + 4) % LANES, 1), s)
                for v, s in zip(new, second)
            ]
            flux, right, face, c0, c1, c2 = flux_next, right_next, face_next, c1, c2, c3
        return (flux, right, face, c0, c1, c2), (first, second)

    m3, m2, m1 = low(0), low(1), low(2)
    c0, c1, c2 = row(0), row(1), row(2)
    face_a = face_of(m3, m2, m1, c0)
    face_b = face_of(m2, m1, c0, c1)
    face_c = face_of(m1, c0, c1, c2)
    _, right_a = edges_of(m1, face_a, face_b)
    left_b, right_b = edges_of(c0, face_b, face_c)
    carry = (flux_of(right_a, left_b, 2), right_b, face_c, c0, c1, c2)
    zeros = [jnp.zeros((8, LANES), jnp.float32) for _ in range(5)]
    half = blocks // 2

    def step(h, state):
        return block(h, state[0], lambda sub: row(4 * h + sub + 3), state[1])

    carry, packed = lax.fori_loop(0, half, step, (carry, (zeros, zeros)))
    for k in range(5):
        edge_ref[0, 0, k] = packed[0][k]
        edge_ref[1, 0, k] = packed[1][k]
    carry, packed = lax.fori_loop(half, blocks - 1, step, (carry, (zeros, zeros)))

    def last(sub):
        return row(rows_y - 1) if sub == 0 else high(sub - 1)

    carry, packed = block(blocks - 1, carry, last, packed)
    for k in range(5):
        edge_ref[0, 1, k] = packed[0][k]
        edge_ref[1, 1, k] = packed[1][k]


def sweep_y(fluid, low, high, blocks):
    nx, ny, nz = fluid.shape[1:]
    return pl.pallas_call(
        sweep_y_kernel,
        out_shape=(
            jax.ShapeDtypeStruct((blocks, 5, nx * ny // blocks, nz), jnp.float32),
            jax.ShapeDtypeStruct((2, 2, 5, nx, nz), jnp.float32),
        ),
        in_specs=[pl.BlockSpec(memory_space=pltpu.VMEM)] * 3,
        out_specs=(pl.BlockSpec(memory_space=pltpu.VMEM),) * 2,
        compiler_params=pltpu.CompilerParams(vmem_limit_bytes=16 * 1024 * 1024),
        cost_estimate=pl.CostEstimate(
            flops=20_000_000, bytes_accessed=2_700_000, transcendentals=0
        ),
        name="sweep_y",
    )(fluid.reshape(5, nx * ny, nz), low, high)


def sweep_z_kernel(lines_ref, out_ref):
    tiles = lines_ref.shape[0]
    lane = lax.broadcasted_iota(jnp.int32, (8, LANES), 1)
    memo = {}

    def once(fn):
        def cached(t):
            key = (fn.__name__, t % tiles)
            if key not in memo:
                memo[key] = fn(t % tiles)
            return memo[key]

        return cached

    @once
    def cell(t):
        return [lines_ref[t, k] for k in range(5)]

    @once
    def after(t):
        return lane_after(cell(t), cell(t + 1), lane)

    @once
    def face(t):
        second = [
            pltpu.roll(jnp.where(lane < 2, f, h), LANES - 2, 1)
            for h, f in zip(cell(t), cell(t + 1))
        ]
        return face_of(lane_before(cell(t), cell(t - 1), lane), cell(t), after(t), second)

    @once
    def edges(t):
        return edges_of(cell(t), lane_before(face(t), face(t - 1), lane), face(t))

    @once
    def flux(t):
        return flux_of(edges(t)[1], lane_after(edges(t)[0], edges(t + 1)[0], lane), 3)

    for t in range(tiles):
        new = updated(cell(t), lane_before(flux(t), flux(t - 1), lane), flux(t))
        for k in range(5):
            for half in range(2):
                out_ref[k, half, :, t * LANES : (t + 1) * LANES] = new[k][4 * half : 4 * half + 4]


def sweep_z(lines, nx):
    tiles, _, rows, _ = lines.shape
    sub = rows // nx
    return pl.pallas_call(
        sweep_z_kernel,
        grid=(rows // 8,),
        out_shape=jax.ShapeDtypeStruct((5, nx, sub, tiles * LANES), jnp.float32),
        in_specs=[pl.BlockSpec((tiles, 5, 8, LANES), lambda q: (0, 0, q, 0))],
        out_specs=pl.BlockSpec((5, 2, sub, tiles * LANES), lambda q: (0, q, 0, 0)),
        compiler_params=pltpu.CompilerParams(vmem_limit_bytes=16 * 1024 * 1024),
        cost_estimate=pl.CostEstimate(
            flops=20_000_000, bytes_accessed=2_700_000, transcendentals=0
        ),
        name="sweep_z",
    )(lines)


def tracers_kernel(owner_ref, count_ref, middle_ref, low_ref, high_ref, cell_ref, peak_ref,
                   out_ref, press_ref):
    blocks, _, rows, _ = middle_ref.shape
    lane = lax.broadcasted_iota(jnp.int32, (8, LANES), 1)

    def owner_rows(h, _):
        for sub in range(4):
            spot = 4 * (h * 4 + sub)
            part = spot // LANES
            spot = spot % LANES
            here = [middle_ref[h, k, pl.ds(sub, 8, stride=4), :] for k in range(5)]
            prev = [pltpu.roll(low_ref[part, k], (2 * LANES - 4 - spot) % LANES, 1) for k in range(5)]
            foll = [pltpu.roll(high_ref[part, k], (LANES - spot) % LANES, 1) for k in range(5)]
            second = [
                pltpu.roll(jnp.where(lane < 2, f, c), LANES - 2, 1) for c, f in zip(here, foll)
            ]
            after = lane_after(here, foll, lane)
            face = face_of(lane_before(here, prev, lane), here, after, second)
            face_prev = face_of(
                [pltpu.roll(c, 1, 1) for c in prev],
                prev,
                lane_after(prev, here, lane),
                [pltpu.roll(jnp.where(lane < 2, c, p), LANES - 2, 1) for p, c in zip(prev, here)],
            )
            face_foll = face_of(
                lane_before(foll, here, lane),
                foll,
                [pltpu.roll(c, LANES - 1, 1) for c in foll],
                [pltpu.roll(c, LANES - 2, 1) for c in foll],
            )
            left, right = edges_of(here, lane_before(face, face_prev, lane), face)
            _, right_prev = edges_of(
                prev, [pltpu.roll(c, 1, 1) for c in face_prev], face_prev
            )
            left_foll, _ = edges_of(foll, lane_before(face_foll, face, lane), face_foll)
            flux = flux_of(right, lane_after(left, left_foll, lane), 3)
            flux_prev = flux_of(right_prev, lane_after(right_prev, left, lane), 3)
            new = updated(here, lane_before(flux, flux_prev, lane), flux)
            press_ref[h, pl.ds(sub, 8, stride=4), :] = new[4]
        return 0

    lax.fori_loop(0, blocks, owner_rows, 0)
    row_ids = lax.broadcasted_iota(jnp.int32, (rows, LANES), 0)
    lane_row = lax.broadcasted_iota(jnp.int32, (1, LANES), 1)
    for j in range(blocks):
        cells = cell_ref[j : j + 1, :]
        table = press_ref[owner_ref[j]]
        z_ids = jnp.broadcast_to(cells % LANES, (rows, LANES))
        picked = jnp.take_along_axis(table, z_ids, axis=1, mode="promise_in_bounds")
        chosen = jnp.broadcast_to(cells // LANES, (rows, LANES)) == row_ids
        sampled = jnp.sum(jnp.where(chosen, picked, 0.0), axis=0, keepdims=True)
        raised = jnp.maximum(peak_ref[j : j + 1, :], sampled)
        out_ref[j : j + 1, :] = jnp.where(lane_row < count_ref[j], raised, 0.0)


def tracers(middle, low, high, owner, count, cells, peaks):
    blocks, _, rows, _ = middle.shape
    return pl.pallas_call(
        tracers_kernel,
        out_shape=jax.ShapeDtypeStruct(peaks.shape, jnp.float32),
        in_specs=[pl.BlockSpec(memory_space=pltpu.SMEM)] * 2
        + [pl.BlockSpec(memory_space=pltpu.VMEM)] * 5,
        out_specs=pl.BlockSpec(memory_space=pltpu.VMEM),
        scratch_shapes=[pltpu.VMEM((blocks, rows, LANES), jnp.float32)],
        compiler_params=pltpu.CompilerParams(vmem_limit_bytes=16 * 1024 * 1024),
        cost_estimate=pl.CostEstimate(
            flops=60_000_000, bytes_accessed=1_400_000, transcendentals=0
        ),
        name="tracers",
    )(owner, count, middle, low, high, cells, peaks)


def shifted(values, axis, step):
    count = lax.axis_size(axis)
    return lax.ppermute(values, axis, [(i, (i + step) % count) for i in range(count)])


def on_device(fluid_state, tracer_cell, tracer_owner, tracer_count, tracer_peak):
    nx, ny = fluid_state.shape[1:3]
    blocks = lax.axis_size("gz")
    head = jnp.transpose(fluid_state[:, :, :3], (2, 0, 1, 3))
    tail = jnp.transpose(fluid_state[:, :, ny - 3 :], (2, 0, 1, 3))
    low = shifted(tail, "gy", 1)
    high = shifted(head, "gy", -1)
    middle, edge = sweep_y(fluid_state, low, high, blocks)
    lines = lax.all_to_all(middle, "gz", split_axis=0, concat_axis=0, tiled=True)
    z_high = shifted(edge[0], "gz", -1)
    z_low = shifted(edge[1], "gz", 1)
    new_peak = tracers(
        middle, z_low, z_high, tracer_owner[0, 0], tracer_count[0, 0], tracer_cell[0, 0],
        tracer_peak[0, 0],
    )
    new_state = sweep_z(lines, nx)
    return (new_state, new_peak[None, None])


def solution(mesh):
    in_specs = (
        P(None, None, "gy", "gz"),
        P("gy", "gz", None, None),
        P("gy", "gz", None),
        P("gy", "gz", None),
        P("gy", "gz", None, None),
    )
    out_specs = (P(None, None, ("gy", "gz"), None), P("gy", "gz", None, None))
    return jax.shard_map(
        on_device, mesh=mesh, in_specs=in_specs, out_specs=out_specs, check_vma=False
    )
```

```python
import jax
import jax.numpy as jnp
from jax import lax
from jax.experimental import pallas as pl
from jax.experimental.pallas import tpu as pltpu
from jax.sharding import PartitionSpec as P

GAMMA = 1.4
RATIO = 0.06
LANES = 128


def median_of(first, second, third):
    return jnp.maximum(jnp.minimum(first, second), jnp.minimum(jnp.maximum(first, second), third))


def face_of(before, left, right, after):
    out = []
    for b, l, r, a in zip(before, left, right, after):
        mid = (7.0 / 12.0) * (l + r) - (1.0 / 12.0) * (b + a)
        out.append(jnp.minimum(jnp.maximum(mid, jnp.minimum(l, r)), jnp.maximum(l, r)))
    return out


def edges_of(centre, face_left, face_right):
    left, right = [], []
    for a, fl, fr in zip(centre, face_left, face_right):
        triple = 3.0 * a
        left.append(median_of(a, fl, triple - 2.0 * fr))
        right.append(median_of(a, fr, triple - 2.0 * fl))
    return left, right


def inverse(value):
    return pl.reciprocal(value, approx=True)


def sound(rho, p):
    heat = GAMMA * p
    return heat * lax.rsqrt(jnp.maximum(heat * rho, 1e-30))


def flux_of(left, right, normal):
    rho_l, p_l, u_l = left[0], left[4], left[normal]
    rho_r, p_r, u_r = right[0], right[4], right[normal]
    c_l = sound(rho_l, p_l)
    c_r = sound(rho_r, p_r)
    slow = jnp.minimum(jnp.minimum(u_l - c_l, u_r - c_r), 0.0)
    fast = jnp.maximum(jnp.maximum(u_l + c_l, u_r + c_r), 0.0)
    scale = RATIO * inverse(fast - slow)
    a_l = fast * scale
    a_r = slow * scale
    w_l = a_l * (u_l - slow)
    w_r = a_r * (u_r - fast)
    q_l = rho_l * w_l
    q_r = rho_r * w_r
    flux = [q_l - q_r] + [q_l * left[k] - q_r * right[k] for k in (1, 2, 3)]
    push_l = a_l * p_l
    push_r = a_r * p_r
    flux[normal] = flux[normal] + (push_l - push_r)
    square_l = left[1] * left[1] + left[2] * left[2] + left[3] * left[3]
    square_r = right[1] * right[1] + right[2] * right[2] + right[3] * right[3]
    flux.append(
        0.2 * (q_l * square_l - q_r * square_r)
        + 0.4 * (push_l * u_l - push_r * u_r)
        + (p_l * w_l - p_r * w_r)
    )
    return flux


def updated(state, flux_left, flux_right):
    rho, vx, vy, vz, p = state
    change = [r - l for l, r in zip(flux_left, flux_right)]
    mom = [rho * v for v in (vx, vy, vz)]
    twice = mom[0] * vx + mom[1] * vy + mom[2] * vz
    rho_new = rho - change[0]
    mom_new = [m - d for m, d in zip(mom, change[1:4])]
    inv = inverse(rho_new)
    vel = [m * inv for m in mom_new]
    twice_new = mom_new[0] * vel[0] + mom_new[1] * vel[1] + mom_new[2] * vel[2]
    return [rho_new] + vel + [p - change[4] + 0.2 * (twice - twice_new)]


def lane_after(here, following, lane):
    return [
        pltpu.roll(jnp.where(lane == 0, f, h), LANES - 1, 1) for h, f in zip(here, following)
    ]


def lane_before(here, previous, lane):
    return [
        pltpu.roll(jnp.where(lane == LANES - 1, p, h), 1, 1) for h, p in zip(here, previous)
    ]


def sweep_y_kernel(fluid_ref, low_ref, high_ref, middle_ref, cells_ref, new_ref, in_sem, out_sem):
    nx, rows_y = fluid_ref.shape[1:3]
    blocks = middle_ref.shape[0]
    chunks = 4
    depth = rows_y // chunks
    copies = []
    for c in range(chunks):
        part = pl.ds(c * depth, depth)
        copies.append(
            pltpu.make_async_copy(
                fluid_ref.at[:, :, part, :], cells_ref.at[:, :, part, :], in_sem.at[c]
            )
        )
        copies[c].start()
    flat_ref = cells_ref.reshape(5, nx * rows_y, LANES)

    def row(y):
        return [flat_ref[k, pl.ds(y, nx, stride=rows_y), :] for k in range(5)]

    def low(i):
        return [low_ref[i, k] for k in range(5)]

    def high(i):
        return [high_ref[i, k] for k in range(5)]

    def block(h, carry, load):
        flux, right, face, c0, c1, c2 = carry
        for sub in range(4):
            c3 = load(sub)
            face_next = face_of(c0, c1, c2, c3)
            left_next, right_next = edges_of(c1, face, face_next)
            flux_next = flux_of(right, left_next, 2)
            new = updated(c0, flux, flux_next)
            for k in range(5):
                new_ref[h, k, pl.ds(sub, 8, stride=4), :] = new[k]
            flux, right, face, c0, c1, c2 = flux_next, right_next, face_next, c1, c2, c3
        return flux, right, face, c0, c1, c2

    def step(h, carry):
        return block(h, carry, lambda sub: row(4 * h + sub + 3))

    def send(i, first, count):
        part = pl.ds(first, count)
        copy = pltpu.make_async_copy(new_ref.at[part], middle_ref.at[part], out_sem.at[i])
        copy.start()
        return copy

    copies[0].wait()
    m3, m2, m1 = low(0), low(1), low(2)
    c0, c1, c2 = row(0), row(1), row(2)
    face_a = face_of(m3, m2, m1, c0)
    face_b = face_of(m2, m1, c0, c1)
    face_c = face_of(m1, c0, c1, c2)
    _, right_a = edges_of(m1, face_a, face_b)
    left_b, right_b = edges_of(c0, face_b, face_c)
    carry = (flux_of(right_a, left_b, 2), right_b, face_c, c0, c1, c2)
    first = 0
    sent = []
    for c in range(chunks):
        until = (c + 1) * blocks // chunks - 1
        carry = lax.fori_loop(first, until, step, carry)
        sent.append(send(c, first, until - first))
        first = until
        if c + 1 < chunks:
            copies[c + 1].wait()

    def last(sub):
        return row(rows_y - 1) if sub == 0 else high(sub - 1)

    block(blocks - 1, carry, last)
    sent.append(send(chunks, blocks - 1, 1))
    for copy in sent:
        copy.wait()


def sweep_y(fluid, low, high, blocks):
    nx, ny, nz = fluid.shape[1:]
    rows = nx * ny // blocks
    return pl.pallas_call(
        sweep_y_kernel,
        out_shape=jax.ShapeDtypeStruct((blocks, 5, rows, nz), jnp.float32),
        in_specs=[pl.BlockSpec(memory_space=pl.ANY)] + [pl.BlockSpec(memory_space=pltpu.VMEM)] * 2,
        out_specs=pl.BlockSpec(memory_space=pl.ANY),
        scratch_shapes=[
            pltpu.VMEM((5, nx, ny, nz), jnp.float32),
            pltpu.VMEM((blocks, 5, rows, nz), jnp.float32),
            pltpu.SemaphoreType.DMA((4,)),
            pltpu.SemaphoreType.DMA((5,)),
        ],
        compiler_params=pltpu.CompilerParams(vmem_limit_bytes=16 * 1024 * 1024),
        cost_estimate=pl.CostEstimate(
            flops=20_000_000, bytes_accessed=2_700_000, transcendentals=0
        ),
        name="sweep_y",
    )(fluid, low, high)


def sweep_z_kernel(lines_ref, out_ref, face_ref, left_ref, right_ref, flux_ref):
    tiles = lines_ref.shape[0]
    lane = lax.broadcasted_iota(jnp.int32, (8, LANES), 1)

    spot = pl.multiple_of(pl.program_id(0) * 8, 8)

    def get(ref, t):
        if ref is lines_ref:
            return [ref[t % tiles, k, pl.ds(spot, 8), :] for k in range(5)]
        return [ref[t % tiles, k] for k in range(5)]

    def put(ref, t, values):
        for k in range(5):
            ref[t, k] = values[k]

    for t in range(tiles):
        before, here, following = [get(lines_ref, t + d) for d in (-1, 0, 1)]
        second = [
            pltpu.roll(jnp.where(lane < 2, f, h), LANES - 2, 1) for h, f in zip(here, following)
        ]
        put(face_ref, t, face_of(
            lane_before(here, before, lane), here, lane_after(here, following, lane), second
        ))
    for t in range(tiles):
        face = get(face_ref, t)
        left, right = edges_of(
            get(lines_ref, t), lane_before(face, get(face_ref, t - 1), lane), face
        )
        put(left_ref, t, left)
        put(right_ref, t, right)
    for t in range(tiles):
        follow = lane_after(get(left_ref, t), get(left_ref, t + 1), lane)
        put(flux_ref, t, flux_of(get(right_ref, t), follow, 3))
    for t in range(tiles):
        flux = get(flux_ref, t)
        new = updated(get(lines_ref, t), lane_before(flux, get(flux_ref, t - 1), lane), flux)
        for k in range(5):
            for half in range(2):
                out_ref[k, half, :, t * LANES : (t + 1) * LANES] = new[k][4 * half : 4 * half + 4]


def sweep_z(lines, nx):
    tiles, _, rows, _ = lines.shape
    sub = rows // nx
    return pl.pallas_call(
        sweep_z_kernel,
        grid=(rows // 8,),
        out_shape=jax.ShapeDtypeStruct((5, nx, sub, tiles * LANES), jnp.float32),
        in_specs=[pl.BlockSpec(memory_space=pltpu.VMEM)],
        out_specs=pl.BlockSpec((5, 2, sub, tiles * LANES), lambda q: (0, q, 0, 0)),
        scratch_shapes=[pltpu.VMEM((tiles, 5, 8, LANES), jnp.float32)] * 4,
        compiler_params=pltpu.CompilerParams(vmem_limit_bytes=16 * 1024 * 1024),
        cost_estimate=pl.CostEstimate(
            flops=20_000_000, bytes_accessed=2_700_000, transcendentals=0
        ),
        name="sweep_z",
    )(lines)


def lines_of(states):
    def after(values):
        return [pltpu.roll(v, LANES - 1, 1) for v in values]

    def before(values):
        return [pltpu.roll(v, 1, 1) for v in values]

    nexts = [after(s) for s in states]
    faces = [face_of(before(s), s, n, after(n)) for s, n in zip(states, nexts)]
    edges = [edges_of(s, before(f), f) for s, f in zip(states, faces)]
    fluxes = [flux_of(right, after(left), 3) for left, right in edges]
    return [updated(s, before(f), f) for s, f in zip(states, fluxes)]


def inner_kernel(owner_ref, middle_ref, cell_ref, sample_ref, edge_ref, low_ref, high_ref, press_ref):
    blocks, _, rows, _ = middle_ref.shape
    lane = lax.broadcasted_iota(jnp.int32, (8, LANES), 1)

    def eight(j, _):
        ends = [jnp.zeros((8, LANES), jnp.float32) for _ in range(5)]
        for part in range(2):
            h = 2 * j + part
            states = [
                [middle_ref[h, k, pl.ds(sub, 8, stride=4), :] for k in range(5)] for sub in range(4)
            ]
            for sub, new in enumerate(lines_of(states)):
                press_ref[h, pl.ds(sub, 8, stride=4), :] = new[4]
            for sub, state in enumerate(states):
                g = 4 * part + sub
                ends = [
                    jnp.where(lane // 16 == g, pltpu.roll(v, (16 * g + 8) % LANES, 1), e)
                    for v, e in zip(state, ends)
                ]
        for k in range(5):
            edge_ref[j, k] = ends[k]
        return 0

    lax.fori_loop(0, blocks // 2, eight, 0)
    for part in range(blocks // 8):
        for k in range(5):
            low = edge_ref[4 * part, k]
            high = low
            for r in range(4):
                ends = edge_ref[4 * part + r, k]
                mine = lane % 16 // 4 == r
                low = jnp.where(mine, pltpu.roll(ends, (LANES + 4 * r - 8) % LANES, 1), low)
                high = jnp.where(mine, pltpu.roll(ends, (LANES + 4 * r - 4) % LANES, 1), high)
            low_ref[part, k] = low
            high_ref[part, k] = high
    row_ids = lax.broadcasted_iota(jnp.int32, (rows, LANES), 0)
    for j in range(blocks):
        cells = cell_ref[j : j + 1, :]
        z_ids = jnp.broadcast_to(cells % LANES, (rows, LANES))
        picked = jnp.take_along_axis(
            press_ref[owner_ref[j]], z_ids, axis=1, mode="promise_in_bounds"
        )
        chosen = jnp.broadcast_to(cells // LANES, (rows, LANES)) == row_ids
        sample_ref[j : j + 1, :] = jnp.sum(jnp.where(chosen, picked, 0.0), axis=0, keepdims=True)


def inner_samples(owner, middle, cells):
    blocks, _, rows, _ = middle.shape
    parts = blocks // 8
    return pl.pallas_call(
        inner_kernel,
        out_shape=(
            jax.ShapeDtypeStruct(cells.shape, jnp.float32),
            jax.ShapeDtypeStruct((blocks // 2, 5, 8, LANES), jnp.float32),
            jax.ShapeDtypeStruct((parts, 5, 8, LANES), jnp.float32),
            jax.ShapeDtypeStruct((parts, 5, 8, LANES), jnp.float32),
        ),
        in_specs=[pl.BlockSpec(memory_space=pltpu.SMEM)]
        + [pl.BlockSpec(memory_space=pltpu.VMEM)] * 2,
        out_specs=(pl.BlockSpec(memory_space=pltpu.VMEM),) * 4,
        scratch_shapes=[pltpu.VMEM((blocks, rows, LANES), jnp.float32)],
        compiler_params=pltpu.CompilerParams(vmem_limit_bytes=16 * 1024 * 1024),
        cost_estimate=pl.CostEstimate(
            flops=20_000_000, bytes_accessed=1_600_000, transcendentals=0
        ),
        name="inner_samples",
    )(owner, middle, cells)


def tracers_kernel(owner_ref, count_ref, sample_ref, edge_ref, low_ref, high_ref, cell_ref, peak_ref,
                   out_ref, table_ref):
    blocks = sample_ref.shape[0]
    lane = lax.broadcasted_iota(jnp.int32, (8, LANES), 1)
    upper = lane % 16 < 8
    batch = 8
    for start in range(0, blocks // 2, batch):
        states = []
        for j in range(start, start + batch):
            part, r = j // 4, j % 4
            ends = [edge_ref[j, k] for k in range(5)]
            below = [pltpu.roll(low_ref[part, k], (LANES + 4 - 4 * r) % LANES, 1) for k in range(5)]
            above = [pltpu.roll(high_ref[part, k], (LANES + 8 - 4 * r) % LANES, 1) for k in range(5)]
            states.append([jnp.where(upper, b, e) for b, e in zip(below, ends)])
            states.append([jnp.where(upper, e, a) for a, e in zip(above, ends)])
        new = lines_of(states)
        for i in range(batch):
            table_ref[start + i] = jnp.where(upper, new[2 * i + 1][4], new[2 * i][4])
    planes = lax.broadcasted_iota(jnp.int32, (8, LANES), 0)
    cells = cell_ref[...]
    z_ids = cells % LANES
    outer = (z_ids < 3) | (z_ids >= LANES - 3)
    sampled = []
    for j in range(blocks):
        owner = owner_ref[j]
        ids = 16 * (4 * (owner % 2) + cells[j : j + 1] // LANES % 4) + (z_ids[j : j + 1] + 8) % 16
        ids = jnp.broadcast_to(ids, (8, LANES))
        picked = jnp.take_along_axis(table_ref[owner // 2], ids, axis=1, mode="promise_in_bounds")
        chosen = jnp.broadcast_to(cells[j : j + 1] // (4 * LANES), (8, LANES)) == planes
        sampled.append(jnp.sum(jnp.where(chosen, picked, 0.0), axis=0, keepdims=True))
    sampled = jnp.where(outer, jnp.concatenate(sampled, axis=0), sample_ref[...])
    slot = lax.broadcasted_iota(jnp.int32, (1, LANES), 1)
    raised = jnp.maximum(peak_ref[...], sampled)
    for j in range(blocks):
        out_ref[j : j + 1, :] = jnp.where(slot < count_ref[j], raised[j : j + 1, :], 0.0)


def tracers(owner, count, sample, edge, low, high, cells, peaks):
    blocks = sample.shape[0]
    return pl.pallas_call(
        tracers_kernel,
        out_shape=jax.ShapeDtypeStruct(peaks.shape, jnp.float32),
        in_specs=[pl.BlockSpec(memory_space=pltpu.SMEM)] * 2
        + [pl.BlockSpec(memory_space=pltpu.VMEM)] * 6,
        out_specs=pl.BlockSpec(memory_space=pltpu.VMEM),
        scratch_shapes=[pltpu.VMEM((blocks // 2, 8, LANES), jnp.float32)],
        compiler_params=pltpu.CompilerParams(vmem_limit_bytes=16 * 1024 * 1024),
        cost_estimate=pl.CostEstimate(
            flops=5_000_000, bytes_accessed=800_000, transcendentals=0
        ),
        name="tracers",
    )(owner, count, sample, edge, low, high, cells, peaks)


def shifted(values, axis, step):
    count = lax.axis_size(axis)
    return lax.ppermute(values, axis, [(i, (i + step) % count) for i in range(count)])


def on_device(fluid_state, tracer_cell, tracer_owner, tracer_count, tracer_peak):
    nx, ny = fluid_state.shape[1:3]
    blocks = lax.axis_size("gz")
    head = jnp.transpose(fluid_state[:, :, :3], (2, 0, 1, 3))
    tail = jnp.transpose(fluid_state[:, :, ny - 3 :], (2, 0, 1, 3))
    low = shifted(tail, "gy", 1)
    high = shifted(head, "gy", -1)
    middle = sweep_y(fluid_state, low, high, blocks)
    lines = lax.all_to_all(middle, "gz", split_axis=0, concat_axis=0, tiled=True)
    owner, cells = tracer_owner[0, 0], tracer_cell[0, 0]
    sample, edge, z_head, z_tail = inner_samples(owner, middle, cells)
    above = shifted(z_head, "gz", -1)
    below = shifted(z_tail, "gz", 1)
    new_peak = tracers(
        owner, tracer_count[0, 0], sample, edge, below, above, cells, tracer_peak[0, 0]
    )
    new_state = sweep_z(lines, nx)
    return (new_state, new_peak[None, None])


def solution(mesh):
    in_specs = (
        P(None, None, "gy", "gz"),
        P("gy", "gz", None, None),
        P("gy", "gz", None),
        P("gy", "gz", None),
        P("gy", "gz", None, None),
    )
    out_specs = (P(None, None, ("gy", "gz"), None), P("gy", "gz", None, None))
    return jax.shard_map(
        on_device, mesh=mesh, in_specs=in_specs, out_specs=out_specs, check_vma=False
    )
```

```python
import jax
import jax.numpy as jnp
from jax import lax
from jax.experimental import pallas as pl
from jax.experimental.pallas import tpu as pltpu
from jax.sharding import PartitionSpec as P

GAMMA = 1.4
RATIO = 0.06
LANES = 128


def median_of(first, second, third):
    return jnp.maximum(jnp.minimum(first, second), jnp.minimum(jnp.maximum(first, second), third))


def face_of(before, left, right, after):
    out = []
    for b, l, r, a in zip(before, left, right, after):
        mid = (7.0 / 12.0) * (l + r) - (1.0 / 12.0) * (b + a)
        out.append(jnp.minimum(jnp.maximum(mid, jnp.minimum(l, r)), jnp.maximum(l, r)))
    return out


def edges_of(centre, face_left, face_right):
    left, right = [], []
    for a, fl, fr in zip(centre, face_left, face_right):
        triple = 3.0 * a
        left.append(median_of(a, fl, triple - 2.0 * fr))
        right.append(median_of(a, fr, triple - 2.0 * fl))
    return left, right


def inverse(value):
    return pl.reciprocal(value, approx=True)


def sound(rho, p):
    heat = GAMMA * p
    return heat * lax.rsqrt(jnp.maximum(heat * rho, 1e-30))


def flux_of(left, right, normal):
    rho_l, p_l, u_l = left[0], left[4], left[normal]
    rho_r, p_r, u_r = right[0], right[4], right[normal]
    c_l = sound(rho_l, p_l)
    c_r = sound(rho_r, p_r)
    slow = jnp.minimum(jnp.minimum(u_l - c_l, u_r - c_r), 0.0)
    fast = jnp.maximum(jnp.maximum(u_l + c_l, u_r + c_r), 0.0)
    scale = RATIO * inverse(fast - slow)
    a_l = fast * scale
    a_r = slow * scale
    w_l = a_l * (u_l - slow)
    w_r = a_r * (u_r - fast)
    q_l = rho_l * w_l
    q_r = rho_r * w_r
    flux = [q_l - q_r] + [q_l * left[k] - q_r * right[k] for k in (1, 2, 3)]
    push_l = a_l * p_l
    push_r = a_r * p_r
    flux[normal] = flux[normal] + (push_l - push_r)
    square_l = left[1] * left[1] + left[2] * left[2] + left[3] * left[3]
    square_r = right[1] * right[1] + right[2] * right[2] + right[3] * right[3]
    flux.append(
        0.2 * (q_l * square_l - q_r * square_r)
        + 0.4 * (push_l * u_l - push_r * u_r)
        + (p_l * w_l - p_r * w_r)
    )
    return flux


def updated(state, flux_left, flux_right):
    rho, vx, vy, vz, p = state
    change = [r - l for l, r in zip(flux_left, flux_right)]
    mom = [rho * v for v in (vx, vy, vz)]
    twice = mom[0] * vx + mom[1] * vy + mom[2] * vz
    rho_new = rho - change[0]
    mom_new = [m - d for m, d in zip(mom, change[1:4])]
    inv = inverse(rho_new)
    vel = [m * inv for m in mom_new]
    twice_new = mom_new[0] * vel[0] + mom_new[1] * vel[1] + mom_new[2] * vel[2]
    return [rho_new] + vel + [p - change[4] + 0.2 * (twice - twice_new)]


def lane_after(here, following, lane):
    return [
        pltpu.roll(jnp.where(lane == 0, f, h), LANES - 1, 1) for h, f in zip(here, following)
    ]


def lane_before(here, previous, lane):
    return [
        pltpu.roll(jnp.where(lane == LANES - 1, p, h), 1, 1) for h, p in zip(here, previous)
    ]


def sweep_y_kernel(fluid_ref, outer_ref, inner_ref, middle_ref, cells_ref, new_ref, in_sem, out_sem):
    nx, rows_y = fluid_ref.shape[1:3]
    blocks = middle_ref.shape[0]
    chunks = 4
    depth = rows_y // chunks
    odd = lax.axis_index("gy") % 2 == 1
    copies = []
    for c in range(chunks):
        part = pl.ds(c * depth, depth)
        copies.append(
            pltpu.make_async_copy(
                fluid_ref.at[:, :, part, :], cells_ref.at[:, :, part, :], in_sem.at[c]
            )
        )
        copies[c].start()
    flat_ref = cells_ref.reshape(5, nx * rows_y, LANES)

    def row(y):
        return [flat_ref[k, pl.ds(y, nx, stride=rows_y), :] for k in range(5)]

    def low(i):
        return [jnp.where(odd, inner_ref[i, k], outer_ref[i, k]) for k in range(5)]

    def high(i):
        return [jnp.where(odd, outer_ref[i, k], inner_ref[i, k]) for k in range(5)]

    def block(h, carry, load):
        flux, right, face, c0, c1, c2 = carry
        for sub in range(4):
            c3 = load(sub)
            face_next = face_of(c0, c1, c2, c3)
            left_next, right_next = edges_of(c1, face, face_next)
            flux_next = flux_of(right, left_next, 2)
            new = updated(c0, flux, flux_next)
            for k in range(5):
                new_ref[h, k, pl.ds(sub, 8, stride=4), :] = new[k]
            flux, right, face, c0, c1, c2 = flux_next, right_next, face_next, c1, c2, c3
        return flux, right, face, c0, c1, c2

    def step(h, carry):
        return block(h, carry, lambda sub: row(4 * h + sub + 3))

    def send(i, first, count):
        part = pl.ds(first, count)
        copy = pltpu.make_async_copy(new_ref.at[part], middle_ref.at[part], out_sem.at[i])
        copy.start()
        return copy

    copies[0].wait()
    m3, m2, m1 = low(0), low(1), low(2)
    c0, c1, c2 = row(0), row(1), row(2)
    face_a = face_of(m3, m2, m1, c0)
    face_b = face_of(m2, m1, c0, c1)
    face_c = face_of(m1, c0, c1, c2)
    _, right_a = edges_of(m1, face_a, face_b)
    left_b, right_b = edges_of(c0, face_b, face_c)
    carry = (flux_of(right_a, left_b, 2), right_b, face_c, c0, c1, c2)
    first = 0
    sent = []
    for c in range(chunks):
        until = (c + 1) * blocks // chunks - 1
        carry = lax.fori_loop(first, until, step, carry, unroll=True)
        sent.append(send(c, first, until - first))
        first = until
        if c + 1 < chunks:
            copies[c + 1].wait()

    def last(sub):
        return row(rows_y - 1) if sub == 0 else high(sub - 1)

    block(blocks - 1, carry, last)
    sent.append(send(chunks, blocks - 1, 1))
    for copy in sent:
        copy.wait()


def sweep_y(fluid, outer, inner, blocks):
    nx, ny, nz = fluid.shape[1:]
    rows = nx * ny // blocks
    return pl.pallas_call(
        sweep_y_kernel,
        out_shape=jax.ShapeDtypeStruct((blocks, 5, rows, nz), jnp.float32),
        in_specs=[pl.BlockSpec(memory_space=pl.ANY)] + [pl.BlockSpec(memory_space=pltpu.VMEM)] * 2,
        out_specs=pl.BlockSpec(memory_space=pl.ANY),
        scratch_shapes=[
            pltpu.VMEM((5, nx, ny, nz), jnp.float32),
            pltpu.VMEM((blocks, 5, rows, nz), jnp.float32),
            pltpu.SemaphoreType.DMA((4,)),
            pltpu.SemaphoreType.DMA((5,)),
        ],
        compiler_params=pltpu.CompilerParams(vmem_limit_bytes=52 * 1024 * 1024),
        cost_estimate=pl.CostEstimate(
            flops=20_000_000, bytes_accessed=2_700_000, transcendentals=0
        ),
        name="sweep_y",
    )(fluid, outer, inner)


def sweep_z_kernel(lines_ref, out_ref, face_ref, left_ref, right_ref, flux_ref, new_ref, out_sem):
    tiles, _, rows, _ = lines_ref.shape
    steps = rows // 8
    lane = lax.broadcasted_iota(jnp.int32, (8, LANES), 1)

    def cell(q, t):
        return [lines_ref[t % tiles, k, pl.ds(8 * q, 8), :] for k in range(5)]

    def get(ref, q, t):
        return [ref[q % 2, t % tiles, k] for k in range(5)]

    def put(ref, q, t, values):
        for k in range(5):
            ref[q % 2, t, k] = values[k]

    def stage_face(q, t):
        before, here, following = [cell(q, t + d) for d in (-1, 0, 1)]
        second = [
            pltpu.roll(jnp.where(lane < 2, f, h), LANES - 2, 1) for h, f in zip(here, following)
        ]
        put(face_ref, q, t, face_of(
            lane_before(here, before, lane), here, lane_after(here, following, lane), second
        ))

    def stage_edges(q, t):
        face = get(face_ref, q, t)
        left, right = edges_of(
            cell(q, t), lane_before(face, get(face_ref, q, t - 1), lane), face
        )
        put(left_ref, q, t, left)
        put(right_ref, q, t, right)

    def stage_flux(q, t):
        follow = lane_after(get(left_ref, q, t), get(left_ref, q, t + 1), lane)
        put(flux_ref, q, t, flux_of(get(right_ref, q, t), follow, 3))

    def stage_new(q, t):
        flux = get(flux_ref, q, t)
        new = updated(cell(q, t), lane_before(flux, get(flux_ref, q, t - 1), lane), flux)
        for k in range(5):
            for half in range(2):
                place = pl.ds(t * LANES, LANES)
                new_ref[k, 2 * q + half, :, place] = new[k][4 * half : 4 * half + 4]

    sent = []
    stages = (stage_face, stage_edges, stage_flux, stage_new)
    for step in range(steps + 3):
        for start in range(0, tiles, 4):
            for age, stage in enumerate(stages):
                q = step - age
                if 0 <= q < steps:
                    for t in range(start, start + 4):
                        stage(q, t)
        q = step - 3
        if q >= 0:
            part = pl.ds(2 * q, 2)
            copy = pltpu.make_async_copy(new_ref.at[:, part], out_ref.at[:, part], out_sem.at[q])
            copy.start()
            sent.append(copy)
    for copy in sent:
        copy.wait()


def sweep_z(lines, nx):
    tiles, _, rows, _ = lines.shape
    shape = (5, nx, rows // nx, tiles * LANES)
    return pl.pallas_call(
        sweep_z_kernel,
        out_shape=jax.ShapeDtypeStruct(shape, jnp.float32),
        in_specs=[pl.BlockSpec(memory_space=pltpu.VMEM)],
        out_specs=pl.BlockSpec(memory_space=pl.ANY),
        scratch_shapes=[pltpu.VMEM((2, tiles, 5, 8, LANES), jnp.float32)] * 4
        + [pltpu.VMEM(shape, jnp.float32), pltpu.SemaphoreType.DMA((rows // 8,))],
        compiler_params=pltpu.CompilerParams(vmem_limit_bytes=16 * 1024 * 1024),
        cost_estimate=pl.CostEstimate(
            flops=20_000_000, bytes_accessed=2_700_000, transcendentals=0
        ),
        name="sweep_z",
    )(lines)


def lines_of(states):
    def after(values):
        return [pltpu.roll(v, LANES - 1, 1) for v in values]

    def before(values):
        return [pltpu.roll(v, 1, 1) for v in values]

    nexts = [after(s) for s in states]
    faces = [face_of(before(s), s, n, after(n)) for s, n in zip(states, nexts)]
    edges = [edges_of(s, before(f), f) for s, f in zip(states, faces)]
    fluxes = [flux_of(right, after(left), 3) for left, right in edges]
    return [updated(s, before(f), f) for s, f in zip(states, fluxes)]


def inner_kernel(owner_ref, middle_ref, cell_ref, sample_ref, own_ref, up_ref, down_ref, press_ref):
    blocks, _, rows, _ = middle_ref.shape
    lane = lax.broadcasted_iota(jnp.int32, (8, LANES), 1)
    lower = lane < LANES // 2

    def line(h, sub, k):
        return middle_ref[h, k, pl.ds(sub, 8, stride=4), :]

    def four(h, _):
        states = [[line(h, sub, k) for k in range(5)] for sub in range(4)]
        for sub, new in enumerate(lines_of(states)):
            press_ref[h, pl.ds(sub, 8, stride=4), :] = new[4]
        return 0

    lax.fori_loop(0, blocks, four, 0)
    ends = list(range(6)) + list(range(LANES - 6, LANES))
    group = 4
    for k in range(5):

        def gather(i, found):
            found = list(found)
            for at in range(4 * group):
                y = 4 * group * i + at
                moved = pltpu.roll(line(group * i + at // 4, at % 4, k), y, 1)
                for n, z in enumerate(ends):
                    found[n] = jnp.where(lane == (y + z) % LANES, moved, found[n])
            return tuple(found)

        zeros = (jnp.zeros((8, LANES), jnp.float32),) * len(ends)
        found = lax.fori_loop(0, blocks // group, gather, zeros)
        low = [pltpu.roll(found[z], (LANES - z) % LANES, 1) for z in range(6)]
        high = [pltpu.roll(found[6 + n], (LANES // 2 + 6 - n) % LANES, 1) for n in range(6)]
        own = high[:3] + [jnp.where(lower, l, h) for l, h in zip(low[:3], high[3:])] + low[3:]
        for j in range(9):
            own_ref[j, k] = own[j]
        turned = [pltpu.roll(v, LANES // 2, 1) for v in (own[3], own[5])]
        up_ref[0, k] = jnp.where(lower, turned[0], own[4])
        down_ref[0, k] = jnp.where(lower, own[4], turned[0])
        up_ref[1, k] = turned[1]
        down_ref[1, k] = turned[1]
    row_ids = lax.broadcasted_iota(jnp.int32, (rows, LANES), 0)
    for j in range(blocks):
        cells = cell_ref[j : j + 1, :]
        z_ids = jnp.broadcast_to(cells % LANES, (rows, LANES))
        picked = jnp.take_along_axis(
            press_ref[owner_ref[j]], z_ids, axis=1, mode="promise_in_bounds"
        )
        chosen = jnp.broadcast_to(cells // LANES, (rows, LANES)) == row_ids
        sample_ref[j : j + 1, :] = jnp.sum(jnp.where(chosen, picked, 0.0), axis=0, keepdims=True)


def inner_samples(owner, middle, cells):
    blocks, _, rows, _ = middle.shape
    return pl.pallas_call(
        inner_kernel,
        out_shape=(
            jax.ShapeDtypeStruct(cells.shape, jnp.float32),
            jax.ShapeDtypeStruct((9, 5, 8, LANES), jnp.float32),
            jax.ShapeDtypeStruct((2, 5, 8, LANES), jnp.float32),
            jax.ShapeDtypeStruct((2, 5, 8, LANES), jnp.float32),
        ),
        in_specs=[pl.BlockSpec(memory_space=pltpu.SMEM)]
        + [pl.BlockSpec(memory_space=pltpu.VMEM)] * 2,
        out_specs=(pl.BlockSpec(memory_space=pltpu.VMEM),) * 4,
        scratch_shapes=[pltpu.VMEM((blocks, rows, LANES), jnp.float32)],
        compiler_params=pltpu.CompilerParams(vmem_limit_bytes=16 * 1024 * 1024),
        cost_estimate=pl.CostEstimate(
            flops=20_000_000, bytes_accessed=1_600_000, transcendentals=0
        ),
        name="inner_samples",
    )(owner, middle, cells)


def tracers_kernel(owner_ref, count_ref, sample_ref, own_ref, below_ref, above_ref, cell_ref, peak_ref,
                   out_ref):
    blocks = sample_ref.shape[0]
    lane = lax.broadcasted_iota(jnp.int32, (8, LANES), 1)
    lower = lane < LANES // 2

    def ends(ref, k):
        first = ref[0, k]
        return [first, pltpu.roll(first, LANES // 2, 1), ref[1, k]]

    states = [[own_ref[j, k] for k in range(5)] for j in range(9)]
    for k in range(5):
        for j, (b, a) in enumerate(zip(ends(below_ref, k), ends(above_ref, k))):
            states[j][k] = jnp.where(lower, b, states[j][k])
            states[6 + j][k] = jnp.where(lower, states[6 + j][k], a)
    faces = [face_of(*states[j : j + 4]) for j in range(6)]
    edges = [edges_of(states[j + 2], faces[j], faces[j + 1]) for j in range(5)]
    fluxes = [flux_of(edges[j][1], edges[j + 1][0], 3) for j in range(4)]
    tables = [updated(states[j + 3], fluxes[j], fluxes[j + 1])[4] for j in range(3)]
    planes = lax.broadcasted_iota(jnp.int32, (8, LANES), 0)
    cells = cell_ref[...]
    z_ids = cells % LANES
    upper = z_ids >= LANES - 3
    place = jnp.where(upper, z_ids - (LANES - 3), z_ids)
    offset = cells // LANES % 4 + jnp.where(upper, LANES // 2, 0)
    sampled = []
    for j in range(blocks):
        ids = jnp.broadcast_to(offset[j : j + 1] + 4 * owner_ref[j], (8, LANES))
        spot = jnp.broadcast_to(place[j : j + 1], (8, LANES))
        picked = [jnp.take_along_axis(t, ids, axis=1, mode="promise_in_bounds") for t in tables]
        value = jnp.where(spot == 0, picked[0], jnp.where(spot == 1, picked[1], picked[2]))
        chosen = jnp.broadcast_to(cells[j : j + 1] // (4 * LANES), (8, LANES)) == planes
        sampled.append(jnp.sum(jnp.where(chosen, value, 0.0), axis=0, keepdims=True))
    sampled = jnp.where(place < 3, jnp.concatenate(sampled, axis=0), sample_ref[...])
    slot = lax.broadcasted_iota(jnp.int32, (1, LANES), 1)
    raised = jnp.maximum(peak_ref[...], sampled)
    for j in range(blocks):
        out_ref[j : j + 1, :] = jnp.where(slot < count_ref[j], raised[j : j + 1, :], 0.0)


def tracers(owner, count, sample, own, below, above, cells, peaks):
    return pl.pallas_call(
        tracers_kernel,
        out_shape=jax.ShapeDtypeStruct(peaks.shape, jnp.float32),
        in_specs=[pl.BlockSpec(memory_space=pltpu.SMEM)] * 2
        + [pl.BlockSpec(memory_space=pltpu.VMEM)] * 6,
        out_specs=pl.BlockSpec(memory_space=pltpu.VMEM),
        compiler_params=pltpu.CompilerParams(vmem_limit_bytes=16 * 1024 * 1024),
        cost_estimate=pl.CostEstimate(
            flops=2_000_000, bytes_accessed=400_000, transcendentals=0
        ),
        name="tracers",
    )(owner, count, sample, own, below, above, cells, peaks)


def shifted(values, axis, step):
    count = lax.axis_size(axis)
    return lax.ppermute(values, axis, [(i, (i + step) % count) for i in range(count)])


def on_device(fluid_state, tracer_cell, tracer_owner, tracer_count, tracer_peak):
    nx, ny = fluid_state.shape[1:3]
    blocks = lax.axis_size("gz")
    head = jnp.transpose(fluid_state[:, :, :3], (2, 0, 1, 3))
    tail = jnp.transpose(fluid_state[:, :, ny - 3 :], (2, 0, 1, 3))
    count = lax.axis_size("gy")
    odd = lax.axis_index("gy") % 2 == 1
    inner = [(i, i ^ 1) for i in range(count)]
    outer = [((i + 1) % count, ((i ^ 1) + 1) % count) for i in range(count)]
    got_inner = lax.ppermute(jnp.where(odd, head, tail), "gy", inner)
    got_outer = lax.ppermute(jnp.where(odd, tail, head), "gy", outer)
    middle = sweep_y(fluid_state, got_outer, got_inner, blocks)
    lines = lax.all_to_all(middle, "gz", split_axis=0, concat_axis=0, tiled=True)
    owner, cells = tracer_owner[0, 0], tracer_cell[0, 0]
    sample, own, up, down = inner_samples(owner, middle, cells)
    above = shifted(down, "gz", -1)
    below = shifted(up, "gz", 1)
    new_peak = tracers(
        owner, tracer_count[0, 0], sample, own, below, above, cells, tracer_peak[0, 0]
    )
    new_state = sweep_z(lines, nx)
    return (new_state, new_peak[None, None])


def solution(mesh):
    in_specs = (
        P(None, None, "gy", "gz"),
        P("gy", "gz", None, None),
        P("gy", "gz", None),
        P("gy", "gz", None),
        P("gy", "gz", None, None),
    )
    out_specs = (P(None, None, ("gy", "gz"), None), P("gy", "gz", None, None))
    return jax.shard_map(
        on_device, mesh=mesh, in_specs=in_specs, out_specs=out_specs, check_vma=False
    )
```

```python
import jax
import jax.numpy as jnp
from jax import lax
from jax.experimental import pallas as pl
from jax.experimental.pallas import tpu as pltpu
from jax.sharding import PartitionSpec as P

GAMMA = 1.4
RATIO = 0.06
LANES = 128


def median_of(first, second, third):
    return jnp.maximum(jnp.minimum(first, second), jnp.minimum(jnp.maximum(first, second), third))


def face_of(before, left, right, after):
    out = []
    for b, l, r, a in zip(before, left, right, after):
        mid = (7.0 / 12.0) * (l + r) - (1.0 / 12.0) * (b + a)
        out.append(jnp.minimum(jnp.maximum(mid, jnp.minimum(l, r)), jnp.maximum(l, r)))
    return out


def edges_of(centre, face_left, face_right):
    left, right = [], []
    for a, fl, fr in zip(centre, face_left, face_right):
        triple = 3.0 * a
        left.append(median_of(a, fl, triple - 2.0 * fr))
        right.append(median_of(a, fr, triple - 2.0 * fl))
    return left, right


def inverse(value):
    return pl.reciprocal(value, approx=True)


def sound(rho, p):
    heat = GAMMA * p
    return heat * lax.rsqrt(jnp.maximum(heat * rho, 1e-30))


def flux_of(left, right, normal):
    rho_l, p_l, u_l = left[0], left[4], left[normal]
    rho_r, p_r, u_r = right[0], right[4], right[normal]
    c_l = sound(rho_l, p_l)
    c_r = sound(rho_r, p_r)
    slow = jnp.minimum(jnp.minimum(u_l - c_l, u_r - c_r), 0.0)
    fast = jnp.maximum(jnp.maximum(u_l + c_l, u_r + c_r), 0.0)
    scale = RATIO * inverse(fast - slow)
    a_l = fast * scale
    a_r = slow * scale
    w_l = a_l * (u_l - slow)
    w_r = a_r * (u_r - fast)
    q_l = rho_l * w_l
    q_r = rho_r * w_r
    flux = [q_l - q_r] + [q_l * left[k] - q_r * right[k] for k in (1, 2, 3)]
    push_l = a_l * p_l
    push_r = a_r * p_r
    flux[normal] = flux[normal] + (push_l - push_r)
    square_l = left[1] * left[1] + left[2] * left[2] + left[3] * left[3]
    square_r = right[1] * right[1] + right[2] * right[2] + right[3] * right[3]
    flux.append(
        0.2 * (q_l * square_l - q_r * square_r)
        + 0.4 * (push_l * u_l - push_r * u_r)
        + (p_l * w_l - p_r * w_r)
    )
    return flux


def updated(state, flux_left, flux_right):
    rho, vx, vy, vz, p = state
    change = [r - l for l, r in zip(flux_left, flux_right)]
    mom = [rho * v for v in (vx, vy, vz)]
    twice = mom[0] * vx + mom[1] * vy + mom[2] * vz
    rho_new = rho - change[0]
    mom_new = [m - d for m, d in zip(mom, change[1:4])]
    inv = inverse(rho_new)
    vel = [m * inv for m in mom_new]
    twice_new = mom_new[0] * vel[0] + mom_new[1] * vel[1] + mom_new[2] * vel[2]
    return [rho_new] + vel + [p - change[4] + 0.2 * (twice - twice_new)]


def lane_after(here, following, lane):
    return [
        pltpu.roll(jnp.where(lane == 0, f, h), LANES - 1, 1) for h, f in zip(here, following)
    ]


def lane_before(here, previous, lane):
    return [
        pltpu.roll(jnp.where(lane == LANES - 1, p, h), 1, 1) for h, p in zip(here, previous)
    ]


def sweep_y_kernel(fluid_ref, outer_ref, inner_ref, middle_ref, new_ref, out_sem):
    nx, rows_y = fluid_ref.shape[1:3]
    blocks = middle_ref.shape[0]
    chunks = 4
    odd = lax.axis_index("gy") % 2 == 1
    flat_ref = fluid_ref.reshape(5, nx * rows_y, LANES)

    def row(y):
        return [flat_ref[k, pl.ds(y, nx, stride=rows_y), :] for k in range(5)]

    def low(i):
        return [jnp.where(odd, inner_ref[i, k], outer_ref[i, k]) for k in range(5)]

    def high(i):
        return [jnp.where(odd, outer_ref[i, k], inner_ref[i, k]) for k in range(5)]

    def block(h, carry, load):
        flux, right, face, c0, c1, c2 = carry
        for sub in range(4):
            c3 = load(sub)
            face_next = face_of(c0, c1, c2, c3)
            left_next, right_next = edges_of(c1, face, face_next)
            flux_next = flux_of(right, left_next, 2)
            new = updated(c0, flux, flux_next)
            for k in range(5):
                new_ref[h, k, pl.ds(sub, 8, stride=4), :] = new[k]
            flux, right, face, c0, c1, c2 = flux_next, right_next, face_next, c1, c2, c3
        return flux, right, face, c0, c1, c2

    def step(h, carry):
        return block(h, carry, lambda sub: row(4 * h + sub + 3))

    def send(i, first, count):
        part = pl.ds(first, count)
        copy = pltpu.make_async_copy(new_ref.at[part], middle_ref.at[part], out_sem.at[i])
        copy.start()
        return copy

    m3, m2, m1 = low(0), low(1), low(2)
    c0, c1, c2 = row(0), row(1), row(2)
    face_a = face_of(m3, m2, m1, c0)
    face_b = face_of(m2, m1, c0, c1)
    face_c = face_of(m1, c0, c1, c2)
    _, right_a = edges_of(m1, face_a, face_b)
    left_b, right_b = edges_of(c0, face_b, face_c)
    carry = (flux_of(right_a, left_b, 2), right_b, face_c, c0, c1, c2)
    first = 0
    sent = []
    for c in range(chunks):
        until = (c + 1) * blocks // chunks - 1
        carry = lax.fori_loop(first, until, step, carry, unroll=True)
        sent.append(send(c, first, until - first))
        first = until

    def last(sub):
        return row(rows_y - 1) if sub == 0 else high(sub - 1)

    block(blocks - 1, carry, last)
    sent.append(send(chunks, blocks - 1, 1))
    for copy in sent:
        copy.wait()


def stage_kernel(fluid_ref, out_ref, sem):
    copy = pltpu.make_async_copy(fluid_ref, out_ref, sem)
    copy.start()
    copy.wait()


def staged(fluid):
    return pl.pallas_call(
        stage_kernel,
        out_shape=jax.ShapeDtypeStruct(fluid.shape, jnp.float32),
        in_specs=[pl.BlockSpec(memory_space=pl.ANY)],
        out_specs=pl.BlockSpec(memory_space=pltpu.VMEM),
        scratch_shapes=[pltpu.SemaphoreType.DMA],
        compiler_params=pltpu.CompilerParams(vmem_limit_bytes=int(51.5 * 1024 * 1024)),
        cost_estimate=pl.CostEstimate(flops=0, bytes_accessed=2_700_000, transcendentals=0),
        name="stage",
    )(fluid)


def sweep_y(fluid, outer, inner, blocks):
    nx, ny, nz = fluid.shape[1:]
    rows = nx * ny // blocks
    return pl.pallas_call(
        sweep_y_kernel,
        out_shape=jax.ShapeDtypeStruct((blocks, 5, rows, nz), jnp.float32),
        in_specs=[pl.BlockSpec(memory_space=pltpu.VMEM)] * 3,
        out_specs=pl.BlockSpec(memory_space=pl.ANY),
        scratch_shapes=[
            pltpu.VMEM((blocks, 5, rows, nz), jnp.float32),
            pltpu.SemaphoreType.DMA((5,)),
        ],
        compiler_params=pltpu.CompilerParams(vmem_limit_bytes=16 * 1024 * 1024),
        cost_estimate=pl.CostEstimate(
            flops=20_000_000, bytes_accessed=2_700_000, transcendentals=0
        ),
        name="sweep_y",
    )(fluid, outer, inner)


def outer_peaks(floor_ref, ids_ref, code_ref, own_ref, below_ref, above_ref, peak_ref):
    lane = lax.broadcasted_iota(jnp.int32, (8, LANES), 1)
    lower = lane < LANES // 2

    def ends(ref, k):
        first = ref[0, k]
        return [first, pltpu.roll(first, LANES // 2, 1), ref[1, k]]

    states = [[own_ref[j, k] for k in range(5)] for j in range(9)]
    for k in range(5):
        for j, (b, a) in enumerate(zip(ends(below_ref, k), ends(above_ref, k))):
            states[j][k] = jnp.where(lower, b, states[j][k])
            states[6 + j][k] = jnp.where(lower, states[6 + j][k], a)
    faces = [face_of(*states[j : j + 4]) for j in range(6)]
    edges = [edges_of(states[j + 2], faces[j], faces[j + 1]) for j in range(5)]
    fluxes = [flux_of(edges[j][1], edges[j + 1][0], 3) for j in range(4)]
    tables = [updated(states[j + 3], fluxes[j], fluxes[j + 1])[4] for j in range(3)]
    planes = lax.broadcasted_iota(jnp.int32, (8, LANES), 0)
    for j in range(floor_ref.shape[0]):
        ids = jnp.broadcast_to(ids_ref[j : j + 1, :], (8, LANES))
        code = jnp.broadcast_to(code_ref[j : j + 1, :], (8, LANES))
        value = jnp.zeros((8, LANES), jnp.float32)
        for n, table in enumerate(tables):
            picked = jnp.take_along_axis(table, ids, axis=1, mode="promise_in_bounds")
            value = jnp.where(code == planes + 8 * n, picked, value)
        raised = jnp.sum(value, axis=0, keepdims=True)
        peak_ref[j : j + 1, :] = jnp.maximum(floor_ref[j : j + 1, :], raised)


def sweep_z_kernel(lines_ref, floor_ref, ids_ref, code_ref, own_ref, below_ref, above_ref, out_ref, peaks_ref,
                   face_ref, left_ref, right_ref, flux_ref, new_ref, peak_ref, out_sem, peak_sem):
    tiles, _, rows, _ = lines_ref.shape
    steps = rows // 8
    lane = lax.broadcasted_iota(jnp.int32, (8, LANES), 1)

    def cell(q, t):
        return [lines_ref[t % tiles, k, pl.ds(8 * q, 8), :] for k in range(5)]

    def get(ref, q, t):
        return [ref[q % 2, t % tiles, k] for k in range(5)]

    def put(ref, q, t, values):
        for k in range(5):
            ref[q % 2, t, k] = values[k]

    def stage_face(q, t):
        before, here, following = [cell(q, t + d) for d in (-1, 0, 1)]
        second = [
            pltpu.roll(jnp.where(lane < 2, f, h), LANES - 2, 1) for h, f in zip(here, following)
        ]
        put(face_ref, q, t, face_of(
            lane_before(here, before, lane), here, lane_after(here, following, lane), second
        ))

    def stage_edges(q, t):
        face = get(face_ref, q, t)
        left, right = edges_of(
            cell(q, t), lane_before(face, get(face_ref, q, t - 1), lane), face
        )
        put(left_ref, q, t, left)
        put(right_ref, q, t, right)

    def stage_flux(q, t):
        follow = lane_after(get(left_ref, q, t), get(left_ref, q, t + 1), lane)
        put(flux_ref, q, t, flux_of(get(right_ref, q, t), follow, 3))

    def stage_new(q, t):
        flux = get(flux_ref, q, t)
        new = updated(cell(q, t), lane_before(flux, get(flux_ref, q, t - 1), lane), flux)
        for k in range(5):
            for half in range(2):
                place = pl.ds(t * LANES, LANES)
                new_ref[k, 2 * q + half, :, place] = new[k][4 * half : 4 * half + 4]

    outer_peaks(floor_ref, ids_ref, code_ref, own_ref, below_ref, above_ref, peak_ref)
    sent = [pltpu.make_async_copy(peak_ref, peaks_ref, peak_sem)]
    stages = (stage_face, stage_edges, stage_flux, stage_new)
    for step in range(steps + 3):
        for start in range(0, tiles, 4):
            for age, stage in enumerate(stages):
                q = step - age
                if 0 <= q < steps:
                    for t in range(start, start + 4):
                        stage(q, t)
        q = step - 3
        if q == 0:
            sent[0].start()
        if q >= 0:
            part = pl.ds(2 * q, 2)
            copy = pltpu.make_async_copy(new_ref.at[:, part], out_ref.at[:, part], out_sem.at[q])
            copy.start()
            sent.append(copy)
    for copy in sent:
        copy.wait()


def sweep_z(lines, floor, ids, code, own, below, above, nx):
    tiles, _, rows, _ = lines.shape
    shape = (5, nx, rows // nx, tiles * LANES)
    return pl.pallas_call(
        sweep_z_kernel,
        out_shape=(
            jax.ShapeDtypeStruct(shape, jnp.float32),
            jax.ShapeDtypeStruct(floor.shape, jnp.float32),
        ),
        in_specs=[pl.BlockSpec(memory_space=pltpu.VMEM)] * 7,
        out_specs=(pl.BlockSpec(memory_space=pl.ANY),) * 2,
        scratch_shapes=[pltpu.VMEM((2, tiles, 5, 8, LANES), jnp.float32)] * 4
        + [
            pltpu.VMEM(shape, jnp.float32),
            pltpu.VMEM(floor.shape, jnp.float32),
            pltpu.SemaphoreType.DMA((rows // 8,)),
            pltpu.SemaphoreType.DMA,
        ],
        compiler_params=pltpu.CompilerParams(vmem_limit_bytes=16 * 1024 * 1024),
        cost_estimate=pl.CostEstimate(
            flops=20_000_000, bytes_accessed=2_700_000, transcendentals=0
        ),
        name="sweep_z",
    )(lines, floor, ids, code, own, below, above)


def lines_of(states):
    def after(values):
        return [pltpu.roll(v, LANES - 1, 1) for v in values]

    def before(values):
        return [pltpu.roll(v, 1, 1) for v in values]

    nexts = [after(s) for s in states]
    faces = [face_of(before(s), s, n, after(n)) for s, n in zip(states, nexts)]
    edges = [edges_of(s, before(f), f) for s, f in zip(states, faces)]
    fluxes = [flux_of(right, after(left), 3) for left, right in edges]
    return [updated(s, before(f), f) for s, f in zip(states, fluxes)]


def inner_kernel(owner_ref, count_ref, middle_ref, cell_ref, peak_ref, floor_ref, ids_ref, code_ref, own_ref,
                 up_ref, down_ref, press_ref):
    blocks, _, rows, _ = middle_ref.shape
    lane = lax.broadcasted_iota(jnp.int32, (8, LANES), 1)
    lower = lane < LANES // 2

    def line(h, sub, k):
        return middle_ref[h, k, pl.ds(sub, 8, stride=4), :]

    def four(h, _):
        states = [[line(h, sub, k) for k in range(5)] for sub in range(4)]
        for sub, new in enumerate(lines_of(states)):
            press_ref[h, pl.ds(sub, 8, stride=4), :] = new[4]
        return 0

    lax.fori_loop(0, blocks, four, 0)
    ends = list(range(6)) + list(range(LANES - 6, LANES))
    group = 4
    for k in range(5):

        def gather(i, found):
            found = list(found)
            for at in range(4 * group):
                y = 4 * group * i + at
                moved = pltpu.roll(line(group * i + at // 4, at % 4, k), y, 1)
                for n, z in enumerate(ends):
                    found[n] = jnp.where(lane == (y + z) % LANES, moved, found[n])
            return tuple(found)

        zeros = (jnp.zeros((8, LANES), jnp.float32),) * len(ends)
        found = lax.fori_loop(0, blocks // group, gather, zeros)
        low = [pltpu.roll(found[z], (LANES - z) % LANES, 1) for z in range(6)]
        high = [pltpu.roll(found[6 + n], (LANES // 2 + 6 - n) % LANES, 1) for n in range(6)]
        own = high[:3] + [jnp.where(lower, l, h) for l, h in zip(low[:3], high[3:])] + low[3:]
        for j in range(9):
            own_ref[j, k] = own[j]
        turned = [pltpu.roll(v, LANES // 2, 1) for v in (own[3], own[5])]
        up_ref[0, k] = jnp.where(lower, turned[0], own[4])
        down_ref[0, k] = jnp.where(lower, own[4], turned[0])
        up_ref[1, k] = turned[1]
        down_ref[1, k] = turned[1]
    row_ids = lax.broadcasted_iota(jnp.int32, (rows, LANES), 0)
    slot = lax.broadcasted_iota(jnp.int32, (1, LANES), 1)
    for j in range(blocks):
        owner = owner_ref[j]
        cells = cell_ref[j : j + 1, :]
        z = cells % LANES
        picked = jnp.take_along_axis(
            press_ref[owner], jnp.broadcast_to(z, (rows, LANES)), axis=1, mode="promise_in_bounds"
        )
        chosen = jnp.broadcast_to(cells // LANES, (rows, LANES)) == row_ids
        sampled = jnp.sum(jnp.where(chosen, picked, 0.0), axis=0, keepdims=True)
        upper = z >= LANES - 3
        outer = upper | (z < 3)
        live = slot < count_ref[j]
        peak = peak_ref[j : j + 1, :]
        raised = jnp.where(outer, peak, jnp.maximum(peak, sampled))
        floor_ref[j : j + 1, :] = jnp.where(live, raised, 0.0)
        ids_ref[j : j + 1, :] = 4 * owner + cells // LANES % 4 + jnp.where(upper, LANES // 2, 0)
        table = jnp.where(upper, z - (LANES - 3), z)
        code_ref[j : j + 1, :] = jnp.where(outer & live, 8 * table + cells // (4 * LANES), -1)


def inner_samples(owner, count, middle, cells, peaks):
    blocks, _, rows, _ = middle.shape
    return pl.pallas_call(
        inner_kernel,
        out_shape=(
            jax.ShapeDtypeStruct(cells.shape, jnp.float32),
            jax.ShapeDtypeStruct(cells.shape, jnp.int32),
            jax.ShapeDtypeStruct(cells.shape, jnp.int32),
            jax.ShapeDtypeStruct((9, 5, 8, LANES), jnp.float32),
            jax.ShapeDtypeStruct((2, 5, 8, LANES), jnp.float32),
            jax.ShapeDtypeStruct((2, 5, 8, LANES), jnp.float32),
        ),
        in_specs=[pl.BlockSpec(memory_space=pltpu.SMEM)] * 2
        + [pl.BlockSpec(memory_space=pltpu.VMEM)] * 3,
        out_specs=(pl.BlockSpec(memory_space=pltpu.VMEM),) * 6,
        scratch_shapes=[pltpu.VMEM((blocks, rows, LANES), jnp.float32)],
        compiler_params=pltpu.CompilerParams(vmem_limit_bytes=16 * 1024 * 1024),
        cost_estimate=pl.CostEstimate(
            flops=20_000_000, bytes_accessed=1_600_000, transcendentals=0
        ),
        name="inner_samples",
    )(owner, count, middle, cells, peaks)


def shifted(values, axis, step):
    count = lax.axis_size(axis)
    return lax.ppermute(values, axis, [(i, (i + step) % count) for i in range(count)])


def on_device(fluid_state, tracer_cell, tracer_owner, tracer_count, tracer_peak):
    nx, ny = fluid_state.shape[1:3]
    blocks = lax.axis_size("gz")
    head = jnp.transpose(fluid_state[:, :, :3], (2, 0, 1, 3))
    tail = jnp.transpose(fluid_state[:, :, ny - 3 :], (2, 0, 1, 3))
    count = lax.axis_size("gy")
    odd = lax.axis_index("gy") % 2 == 1
    inner = [(i, i ^ 1) for i in range(count)]
    outer = [((i + 1) % count, ((i ^ 1) + 1) % count) for i in range(count)]
    got_inner = lax.ppermute(jnp.where(odd, head, tail), "gy", inner)
    got_outer = lax.ppermute(jnp.where(odd, tail, head), "gy", outer)
    middle = sweep_y(staged(fluid_state), got_outer, got_inner, blocks)
    lines = lax.all_to_all(middle, "gz", split_axis=0, concat_axis=0, tiled=True)
    floor, ids, code, own, up, down = inner_samples(
        tracer_owner[0, 0], tracer_count[0, 0], middle, tracer_cell[0, 0], tracer_peak[0, 0]
    )
    above = shifted(down, "gz", -1)
    below = shifted(up, "gz", 1)
    new_state, new_peak = sweep_z(lines, floor, ids, code, own, below, above, nx)
    return (new_state, new_peak[None, None])


def solution(mesh):
    in_specs = (
        P(None, None, "gy", "gz"),
        P("gy", "gz", None, None),
        P("gy", "gz", None),
        P("gy", "gz", None),
        P("gy", "gz", None, None),
    )
    out_specs = (P(None, None, ("gy", "gz"), None), P("gy", "gz", None, None))
    return jax.shard_map(
        on_device, mesh=mesh, in_specs=in_specs, out_specs=out_specs, check_vma=False
    )
```

```python
import jax
import jax.numpy as jnp
from jax import lax
from jax.experimental import pallas as pl
from jax.experimental.pallas import tpu as pltpu
from jax.sharding import PartitionSpec as P

GAMMA = 1.4
RATIO = 0.06
LANES = 128


def median_of(first, second, third):
    return jnp.maximum(jnp.minimum(first, second), jnp.minimum(jnp.maximum(first, second), third))


def face_of(before, left, right, after):
    out = []
    for b, l, r, a in zip(before, left, right, after):
        mid = (7.0 / 12.0) * (l + r) - (1.0 / 12.0) * (b + a)
        out.append(jnp.minimum(jnp.maximum(mid, jnp.minimum(l, r)), jnp.maximum(l, r)))
    return out


def edges_of(centre, face_left, face_right):
    left, right = [], []
    for a, fl, fr in zip(centre, face_left, face_right):
        triple = 3.0 * a
        left.append(median_of(a, fl, triple - 2.0 * fr))
        right.append(median_of(a, fr, triple - 2.0 * fl))
    return left, right


def inverse(value):
    return pl.reciprocal(value, approx=True)


def sound(rho, p):
    heat = GAMMA * p
    return heat * lax.rsqrt(jnp.maximum(heat * rho, 1e-30))


def flux_of(left, right, normal):
    rho_l, p_l, u_l = left[0], left[4], left[normal]
    rho_r, p_r, u_r = right[0], right[4], right[normal]
    c_l = sound(rho_l, p_l)
    c_r = sound(rho_r, p_r)
    slow = jnp.minimum(jnp.minimum(u_l - c_l, u_r - c_r), 0.0)
    fast = jnp.maximum(jnp.maximum(u_l + c_l, u_r + c_r), 0.0)
    scale = RATIO * inverse(fast - slow)
    a_l = fast * scale
    a_r = slow * scale
    w_l = a_l * (u_l - slow)
    w_r = a_r * (u_r - fast)
    q_l = rho_l * w_l
    q_r = rho_r * w_r
    flux = [q_l - q_r] + [q_l * left[k] - q_r * right[k] for k in (1, 2, 3)]
    push_l = a_l * p_l
    push_r = a_r * p_r
    flux[normal] = flux[normal] + (push_l - push_r)
    square_l = left[1] * left[1] + left[2] * left[2] + left[3] * left[3]
    square_r = right[1] * right[1] + right[2] * right[2] + right[3] * right[3]
    flux.append(
        0.2 * (q_l * square_l - q_r * square_r)
        + 0.4 * (push_l * u_l - push_r * u_r)
        + (p_l * w_l - p_r * w_r)
    )
    return flux


def updated(state, flux_left, flux_right):
    rho, vx, vy, vz, p = state
    change = [r - l for l, r in zip(flux_left, flux_right)]
    mom = [rho * v for v in (vx, vy, vz)]
    twice = mom[0] * vx + mom[1] * vy + mom[2] * vz
    rho_new = rho - change[0]
    mom_new = [m - d for m, d in zip(mom, change[1:4])]
    inv = inverse(rho_new)
    vel = [m * inv for m in mom_new]
    twice_new = mom_new[0] * vel[0] + mom_new[1] * vel[1] + mom_new[2] * vel[2]
    return [rho_new] + vel + [p - change[4] + 0.2 * (twice - twice_new)]


def lane_after(here, following, lane):
    return [
        pltpu.roll(jnp.where(lane == 0, f, h), LANES - 1, 1) for h, f in zip(here, following)
    ]


def lane_before(here, previous, lane):
    return [
        pltpu.roll(jnp.where(lane == LANES - 1, p, h), 1, 1) for h, p in zip(here, previous)
    ]


def sweep_y_kernel(fluid_ref, inner_ref, outer_ref, middle_ref, new_ref, out_sem):
    nx, rows_y = fluid_ref.shape[1:3]
    blocks = middle_ref.shape[0]
    chunks = 4
    odd = lax.axis_index("gy") % 2 == 1
    flat_ref = fluid_ref.reshape(5, nx * rows_y, LANES)

    def row(y):
        return [flat_ref[k, pl.ds(y, nx, stride=rows_y), :] for k in range(5)]

    def low(i):
        return [jnp.where(odd, inner_ref[i, k], outer_ref[i, k]) for k in range(5)]

    def high(i):
        return [jnp.where(odd, outer_ref[i, k], inner_ref[i, k]) for k in range(5)]

    def block(h, carry, load):
        flux, right, face, c0, c1, c2 = carry
        for sub in range(4):
            c3 = load(sub)
            face_next = face_of(c0, c1, c2, c3)
            left_next, right_next = edges_of(c1, face, face_next)
            flux_next = flux_of(right, left_next, 2)
            new = updated(c0, flux, flux_next)
            for k in range(5):
                new_ref[h, k, pl.ds(sub, 8, stride=4), :] = new[k]
            flux, right, face, c0, c1, c2 = flux_next, right_next, face_next, c1, c2, c3
        return flux, right, face, c0, c1, c2

    def step(h, carry):
        return block(h, carry, lambda sub: row(4 * h + sub + 3))

    def send(i, first, count):
        part = pl.ds(first, count)
        copy = pltpu.make_async_copy(new_ref.at[part], middle_ref.at[part], out_sem.at[i])
        copy.start()
        return copy

    m3, m2, m1 = low(0), low(1), low(2)
    c0, c1, c2 = row(0), row(1), row(2)
    face_a = face_of(m3, m2, m1, c0)
    face_b = face_of(m2, m1, c0, c1)
    face_c = face_of(m1, c0, c1, c2)
    _, right_a = edges_of(m1, face_a, face_b)
    left_b, right_b = edges_of(c0, face_b, face_c)
    carry = (flux_of(right_a, left_b, 2), right_b, face_c, c0, c1, c2)
    first = 0
    sent = []
    for c in range(chunks):
        until = (c + 1) * blocks // chunks - 1
        carry = lax.fori_loop(first, until, step, carry, unroll=True)
        sent.append(send(c, first, until - first))
        first = until

    def last(sub):
        return row(rows_y - 1) if sub == 0 else high(sub - 1)

    block(blocks - 1, carry, last)
    sent.append(send(chunks, blocks - 1, 1))
    for copy in sent:
        copy.wait()


def stage_kernel(fluid_ref, out_ref, sem):
    copy = pltpu.make_async_copy(fluid_ref, out_ref, sem)
    copy.start()
    copy.wait()


def staged(fluid):
    return pl.pallas_call(
        stage_kernel,
        out_shape=jax.ShapeDtypeStruct(fluid.shape, jnp.float32),
        in_specs=[pl.BlockSpec(memory_space=pl.ANY)],
        out_specs=pl.BlockSpec(memory_space=pltpu.VMEM),
        scratch_shapes=[pltpu.SemaphoreType.DMA],
        compiler_params=pltpu.CompilerParams(vmem_limit_bytes=int(51.5 * 1024 * 1024)),
        cost_estimate=pl.CostEstimate(flops=0, bytes_accessed=2_700_000, transcendentals=0),
        name="stage",
    )(fluid)


def sweep_y(fluid, inner, outer, blocks):
    nx, ny, nz = fluid.shape[1:]
    rows = nx * ny // blocks
    return pl.pallas_call(
        sweep_y_kernel,
        out_shape=jax.ShapeDtypeStruct((blocks, 5, rows, nz), jnp.float32),
        in_specs=[pl.BlockSpec(memory_space=pltpu.VMEM)] * 3,
        out_specs=pl.BlockSpec(memory_space=pl.ANY),
        scratch_shapes=[
            pltpu.VMEM((blocks, 5, rows, nz), jnp.float32),
            pltpu.SemaphoreType.DMA((5,)),
        ],
        compiler_params=pltpu.CompilerParams(vmem_limit_bytes=16 * 1024 * 1024),
        cost_estimate=pl.CostEstimate(
            flops=20_000_000, bytes_accessed=2_700_000, transcendentals=0
        ),
        name="sweep_y",
    )(fluid, inner, outer)


def outer_peaks(floor_ref, ids_ref, code_ref, own_ref, below_ref, above_ref, peak_ref):
    lane = lax.broadcasted_iota(jnp.int32, (8, LANES), 1)
    lower = lane < LANES // 2

    def ends(ref, k):
        first = ref[0, k]
        return [first, pltpu.roll(first, LANES // 2, 1), ref[1, k]]

    states = [[own_ref[j, k] for k in range(5)] for j in range(9)]
    for k in range(5):
        for j, (b, a) in enumerate(zip(ends(below_ref, k), ends(above_ref, k))):
            states[j][k] = jnp.where(lower, b, states[j][k])
            states[6 + j][k] = jnp.where(lower, states[6 + j][k], a)
    faces = [face_of(*states[j : j + 4]) for j in range(6)]
    edges = [edges_of(states[j + 2], faces[j], faces[j + 1]) for j in range(5)]
    fluxes = [flux_of(edges[j][1], edges[j + 1][0], 3) for j in range(4)]
    tables = [updated(states[j + 3], fluxes[j], fluxes[j + 1])[4] for j in range(3)]
    planes = lax.broadcasted_iota(jnp.int32, (8, LANES), 0)
    for j in range(floor_ref.shape[0]):
        ids = jnp.broadcast_to(ids_ref[j : j + 1, :], (8, LANES))
        code = jnp.broadcast_to(code_ref[j : j + 1, :], (8, LANES))
        value = jnp.zeros((8, LANES), jnp.float32)
        for n, table in enumerate(tables):
            picked = jnp.take_along_axis(table, ids, axis=1, mode="promise_in_bounds")
            value = jnp.where(code == planes + 8 * n, picked, value)
        raised = jnp.sum(value, axis=0, keepdims=True)
        peak_ref[j : j + 1, :] = jnp.maximum(floor_ref[j : j + 1, :], raised)


def sweep_z_kernel(lines_ref, floor_ref, ids_ref, code_ref, own_ref, below_ref, above_ref, out_ref, peaks_ref,
                   face_ref, left_ref, right_ref, flux_ref, new_ref, peak_ref, out_sem, peak_sem):
    tiles, _, rows, _ = lines_ref.shape
    steps = rows // 8
    lane = lax.broadcasted_iota(jnp.int32, (8, LANES), 1)

    def cell(q, t):
        return [lines_ref[t % tiles, k, pl.ds(8 * q, 8), :] for k in range(5)]

    def get(ref, q, t):
        return [ref[q % 2, t % tiles, k] for k in range(5)]

    def put(ref, q, t, values):
        for k in range(5):
            ref[q % 2, t, k] = values[k]

    def stage_face(q, t):
        before, here, following = [cell(q, t + d) for d in (-1, 0, 1)]
        second = [
            pltpu.roll(jnp.where(lane < 2, f, h), LANES - 2, 1) for h, f in zip(here, following)
        ]
        put(face_ref, q, t, face_of(
            lane_before(here, before, lane), here, lane_after(here, following, lane), second
        ))

    def stage_edges(q, t):
        face = get(face_ref, q, t)
        left, right = edges_of(
            cell(q, t), lane_before(face, get(face_ref, q, t - 1), lane), face
        )
        put(left_ref, q, t, left)
        put(right_ref, q, t, right)

    def stage_flux(q, t):
        follow = lane_after(get(left_ref, q, t), get(left_ref, q, t + 1), lane)
        put(flux_ref, q, t, flux_of(get(right_ref, q, t), follow, 3))

    def stage_new(q, t):
        flux = get(flux_ref, q, t)
        new = updated(cell(q, t), lane_before(flux, get(flux_ref, q, t - 1), lane), flux)
        for k in range(5):
            for half in range(2):
                place = pl.ds(t * LANES, LANES)
                new_ref[k, 2 * q + half, :, place] = new[k][4 * half : 4 * half + 4]

    outer_peaks(floor_ref, ids_ref, code_ref, own_ref, below_ref, above_ref, peak_ref)
    sent = [pltpu.make_async_copy(peak_ref, peaks_ref, peak_sem)]
    stages = (stage_face, stage_edges, stage_flux, stage_new)
    for step in range(steps + 3):
        for start in range(0, tiles, 4):
            for age, stage in enumerate(stages):
                q = step - age
                if 0 <= q < steps:
                    for t in range(start, start + 4):
                        stage(q, t)
        q = step - 3
        if q == 0:
            sent[0].start()
        if q >= 0:
            part = pl.ds(2 * q, 2)
            copy = pltpu.make_async_copy(new_ref.at[:, part], out_ref.at[:, part], out_sem.at[q])
            copy.start()
            sent.append(copy)
    for copy in sent:
        copy.wait()


def sweep_z(lines, floor, ids, code, own, below, above, nx):
    tiles, _, rows, _ = lines.shape
    shape = (5, nx, rows // nx, tiles * LANES)
    return pl.pallas_call(
        sweep_z_kernel,
        out_shape=(
            jax.ShapeDtypeStruct(shape, jnp.float32),
            jax.ShapeDtypeStruct(floor.shape, jnp.float32),
        ),
        in_specs=[pl.BlockSpec(memory_space=pltpu.VMEM)] * 7,
        out_specs=(pl.BlockSpec(memory_space=pl.ANY),) * 2,
        scratch_shapes=[pltpu.VMEM((2, tiles, 5, 8, LANES), jnp.float32)] * 4
        + [
            pltpu.VMEM(shape, jnp.float32),
            pltpu.VMEM(floor.shape, jnp.float32),
            pltpu.SemaphoreType.DMA((rows // 8,)),
            pltpu.SemaphoreType.DMA,
        ],
        compiler_params=pltpu.CompilerParams(vmem_limit_bytes=16 * 1024 * 1024),
        cost_estimate=pl.CostEstimate(
            flops=20_000_000, bytes_accessed=2_700_000, transcendentals=0
        ),
        name="sweep_z",
    )(lines, floor, ids, code, own, below, above)


def lines_of(states):
    def after(values):
        return [pltpu.roll(v, LANES - 1, 1) for v in values]

    def before(values):
        return [pltpu.roll(v, 1, 1) for v in values]

    nexts = [after(s) for s in states]
    faces = [face_of(before(s), s, n, after(n)) for s, n in zip(states, nexts)]
    edges = [edges_of(s, before(f), f) for s, f in zip(states, faces)]
    fluxes = [flux_of(right, after(left), 3) for left, right in edges]
    return [updated(s, before(f), f) for s, f in zip(states, fluxes)]


def inner_kernel(owner_ref, count_ref, middle_ref, cell_ref, peak_ref, floor_ref, ids_ref, code_ref, own_ref,
                 up_ref, down_ref, press_ref):
    blocks, _, rows, _ = middle_ref.shape
    lane = lax.broadcasted_iota(jnp.int32, (8, LANES), 1)
    lower = lane < LANES // 2

    def line(h, sub, k):
        return middle_ref[h, k, pl.ds(sub, 8, stride=4), :]

    def four(h, _):
        states = [[line(h, sub, k) for k in range(5)] for sub in range(4)]
        for sub, new in enumerate(lines_of(states)):
            press_ref[h, pl.ds(sub, 8, stride=4), :] = new[4]
        return 0

    lax.fori_loop(0, blocks, four, 0)
    ends = list(range(6)) + list(range(LANES - 6, LANES))
    group = 4
    for k in range(5):

        def gather(i, found):
            found = list(found)
            for at in range(4 * group):
                y = 4 * group * i + at
                moved = pltpu.roll(line(group * i + at // 4, at % 4, k), y, 1)
                for n, z in enumerate(ends):
                    found[n] = jnp.where(lane == (y + z) % LANES, moved, found[n])
            return tuple(found)

        zeros = (jnp.zeros((8, LANES), jnp.float32),) * len(ends)
        found = lax.fori_loop(0, blocks // group, gather, zeros)
        low = [pltpu.roll(found[z], (LANES - z) % LANES, 1) for z in range(6)]
        high = [pltpu.roll(found[6 + n], (LANES // 2 + 6 - n) % LANES, 1) for n in range(6)]
        own = high[:3] + [jnp.where(lower, l, h) for l, h in zip(low[:3], high[3:])] + low[3:]
        for j in range(9):
            own_ref[j, k] = own[j]
        turned = [pltpu.roll(v, LANES // 2, 1) for v in (own[3], own[5])]
        up_ref[0, k] = jnp.where(lower, turned[0], own[4])
        down_ref[0, k] = jnp.where(lower, own[4], turned[0])
        up_ref[1, k] = turned[1]
        down_ref[1, k] = turned[1]
    row_ids = lax.broadcasted_iota(jnp.int32, (rows, LANES), 0)
    slot = lax.broadcasted_iota(jnp.int32, (1, LANES), 1)
    for j in range(blocks):
        owner = owner_ref[j]
        cells = cell_ref[j : j + 1, :]
        z = cells % LANES
        picked = jnp.take_along_axis(
            press_ref[owner], jnp.broadcast_to(z, (rows, LANES)), axis=1, mode="promise_in_bounds"
        )
        chosen = jnp.broadcast_to(cells // LANES, (rows, LANES)) == row_ids
        sampled = jnp.sum(jnp.where(chosen, picked, 0.0), axis=0, keepdims=True)
        upper = z >= LANES - 3
        outer = upper | (z < 3)
        live = slot < count_ref[j]
        peak = peak_ref[j : j + 1, :]
        raised = jnp.where(outer, peak, jnp.maximum(peak, sampled))
        floor_ref[j : j + 1, :] = jnp.where(live, raised, 0.0)
        ids_ref[j : j + 1, :] = 4 * owner + cells // LANES % 4 + jnp.where(upper, LANES // 2, 0)
        table = jnp.where(upper, z - (LANES - 3), z)
        code_ref[j : j + 1, :] = jnp.where(outer & live, 8 * table + cells // (4 * LANES), -1)


def inner_samples(owner, count, middle, cells, peaks):
    blocks, _, rows, _ = middle.shape
    return pl.pallas_call(
        inner_kernel,
        out_shape=(
            jax.ShapeDtypeStruct(cells.shape, jnp.float32),
            jax.ShapeDtypeStruct(cells.shape, jnp.int32),
            jax.ShapeDtypeStruct(cells.shape, jnp.int32),
            jax.ShapeDtypeStruct((9, 5, 8, LANES), jnp.float32),
            jax.ShapeDtypeStruct((2, 5, 8, LANES), jnp.float32),
            jax.ShapeDtypeStruct((2, 5, 8, LANES), jnp.float32),
        ),
        in_specs=[pl.BlockSpec(memory_space=pltpu.SMEM)] * 2
        + [pl.BlockSpec(memory_space=pltpu.VMEM)] * 3,
        out_specs=(pl.BlockSpec(memory_space=pltpu.VMEM),) * 6,
        scratch_shapes=[pltpu.VMEM((blocks, rows, LANES), jnp.float32)],
        compiler_params=pltpu.CompilerParams(vmem_limit_bytes=16 * 1024 * 1024),
        cost_estimate=pl.CostEstimate(
            flops=20_000_000, bytes_accessed=1_600_000, transcendentals=0
        ),
        name="inner_samples",
    )(owner, count, middle, cells, peaks)


def shifted(values, axis, step):
    count = lax.axis_size(axis)
    return lax.ppermute(values, axis, [(i, (i + step) % count) for i in range(count)])


def on_device(fluid_state, tracer_cell, tracer_owner, tracer_count, tracer_peak):
    nx, ny = fluid_state.shape[1:3]
    blocks = lax.axis_size("gz")
    head = jnp.transpose(fluid_state[:, :, :3], (2, 0, 1, 3))
    tail = jnp.transpose(fluid_state[:, :, ny - 3 :], (2, 0, 1, 3))
    count = lax.axis_size("gy")
    odd = lax.axis_index("gy") % 2 == 1
    inner = [(i, i ^ 1) for i in range(count)]
    outer = [((i + 1) % count, ((i ^ 1) + 1) % count) for i in range(count)]
    got_inner = lax.ppermute(jnp.where(odd, head, tail), "gy", inner)
    got_outer = lax.ppermute(jnp.where(odd, tail, head), "gy", outer)
    middle = sweep_y(staged(fluid_state), got_inner, got_outer, blocks)
    lines = lax.all_to_all(middle, "gz", split_axis=0, concat_axis=0, tiled=True)
    floor, ids, code, own, up, down = inner_samples(
        tracer_owner[0, 0], tracer_count[0, 0], middle, tracer_cell[0, 0], tracer_peak[0, 0]
    )
    above = shifted(down, "gz", -1)
    below = shifted(up, "gz", 1)
    new_state, new_peak = sweep_z(lines, floor, ids, code, own, below, above, nx)
    return (new_state, new_peak[None, None])


def solution(mesh):
    in_specs = (
        P(None, None, "gy", "gz"),
        P("gy", "gz", None, None),
        P("gy", "gz", None),
        P("gy", "gz", None),
        P("gy", "gz", None, None),
    )
    out_specs = (P(None, None, ("gy", "gz"), None), P("gy", "gz", None, None))
    return jax.shard_map(
        on_device, mesh=mesh, in_specs=in_specs, out_specs=out_specs, check_vma=False
    )
```

```python
import jax
import jax.numpy as jnp
from jax import lax
from jax.experimental import pallas as pl
from jax.experimental.pallas import tpu as pltpu
from jax.sharding import PartitionSpec as P

GAMMA = 1.4
RATIO = 0.06
LANES = 128


def median_of(first, second, third):
    return jnp.maximum(jnp.minimum(first, second), jnp.minimum(jnp.maximum(first, second), third))


def face_of(before, left, right, after):
    out = []
    for b, l, r, a in zip(before, left, right, after):
        mid = (7.0 / 12.0) * (l + r) - (1.0 / 12.0) * (b + a)
        out.append(jnp.minimum(jnp.maximum(mid, jnp.minimum(l, r)), jnp.maximum(l, r)))
    return out


def edges_of(centre, face_left, face_right):
    left, right = [], []
    for a, fl, fr in zip(centre, face_left, face_right):
        triple = 3.0 * a
        left.append(median_of(a, fl, triple - 2.0 * fr))
        right.append(median_of(a, fr, triple - 2.0 * fl))
    return left, right


def inverse(value):
    return pl.reciprocal(value, approx=True)


def sound(rho, p):
    heat = GAMMA * p
    return heat * lax.rsqrt(jnp.maximum(heat * rho, 1e-30))


def flux_of(left, right, normal):
    rho_l, p_l, u_l = left[0], left[4], left[normal]
    rho_r, p_r, u_r = right[0], right[4], right[normal]
    c_l = sound(rho_l, p_l)
    c_r = sound(rho_r, p_r)
    slow = jnp.minimum(jnp.minimum(u_l - c_l, u_r - c_r), 0.0)
    fast = jnp.maximum(jnp.maximum(u_l + c_l, u_r + c_r), 0.0)
    scale = RATIO * inverse(fast - slow)
    a_l = fast * scale
    a_r = slow * scale
    w_l = a_l * (u_l - slow)
    w_r = a_r * (u_r - fast)
    q_l = rho_l * w_l
    q_r = rho_r * w_r
    flux = [q_l - q_r] + [q_l * left[k] - q_r * right[k] for k in (1, 2, 3)]
    push_l = a_l * p_l
    push_r = a_r * p_r
    flux[normal] = flux[normal] + (push_l - push_r)
    square_l = left[1] * left[1] + left[2] * left[2] + left[3] * left[3]
    square_r = right[1] * right[1] + right[2] * right[2] + right[3] * right[3]
    flux.append(
        0.2 * (q_l * square_l - q_r * square_r)
        + 0.4 * (push_l * u_l - push_r * u_r)
        + (p_l * w_l - p_r * w_r)
    )
    return flux


def updated(state, flux_left, flux_right):
    rho, vx, vy, vz, p = state
    change = [r - l for l, r in zip(flux_left, flux_right)]
    mom = [rho * v for v in (vx, vy, vz)]
    twice = mom[0] * vx + mom[1] * vy + mom[2] * vz
    rho_new = rho - change[0]
    mom_new = [m - d for m, d in zip(mom, change[1:4])]
    inv = inverse(rho_new)
    vel = [m * inv for m in mom_new]
    twice_new = mom_new[0] * vel[0] + mom_new[1] * vel[1] + mom_new[2] * vel[2]
    return [rho_new] + vel + [p - change[4] + 0.2 * (twice - twice_new)]


def lane_after(here, following, lane):
    return [
        pltpu.roll(jnp.where(lane == 0, f, h), LANES - 1, 1) for h, f in zip(here, following)
    ]


def lane_before(here, previous, lane):
    return [
        pltpu.roll(jnp.where(lane == LANES - 1, p, h), 1, 1) for h, p in zip(here, previous)
    ]


def sweep_y_kernel(fluid_ref, inner_ref, outer_ref, middle_ref, new_ref, out_sem):
    nx, rows_y = fluid_ref.shape[1:3]
    blocks = middle_ref.shape[0]
    chunks = 4
    odd = lax.axis_index("gy") % 2 == 1
    flat_ref = fluid_ref.reshape(5, nx * rows_y, LANES)

    def row(y):
        return [flat_ref[k, pl.ds(y, nx, stride=rows_y), :] for k in range(5)]

    def low(i):
        return [jnp.where(odd, inner_ref[i, k], outer_ref[i, k]) for k in range(5)]

    def high(i):
        return [jnp.where(odd, outer_ref[i, k], inner_ref[i, k]) for k in range(5)]

    def block(h, carry, load):
        flux, right, face, c0, c1, c2 = carry
        for sub in range(4):
            c3 = load(sub)
            face_next = face_of(c0, c1, c2, c3)
            left_next, right_next = edges_of(c1, face, face_next)
            flux_next = flux_of(right, left_next, 2)
            new = updated(c0, flux, flux_next)
            for k in range(5):
                new_ref[h, k, pl.ds(sub, 8, stride=4), :] = new[k]
            flux, right, face, c0, c1, c2 = flux_next, right_next, face_next, c1, c2, c3
        return flux, right, face, c0, c1, c2

    def step(h, carry):
        return block(h, carry, lambda sub: row(4 * h + sub + 3))

    def send(i, first, count):
        part = pl.ds(first, count)
        copy = pltpu.make_async_copy(new_ref.at[part], middle_ref.at[part], out_sem.at[i])
        copy.start()
        return copy

    m3, m2, m1 = low(0), low(1), low(2)
    c0, c1, c2 = row(0), row(1), row(2)
    face_a = face_of(m3, m2, m1, c0)
    face_b = face_of(m2, m1, c0, c1)
    face_c = face_of(m1, c0, c1, c2)
    _, right_a = edges_of(m1, face_a, face_b)
    left_b, right_b = edges_of(c0, face_b, face_c)
    carry = (flux_of(right_a, left_b, 2), right_b, face_c, c0, c1, c2)
    first = 0
    sent = []
    for c in range(chunks):
        until = (c + 1) * blocks // chunks - 1
        carry = lax.fori_loop(first, until, step, carry, unroll=True)
        sent.append(send(c, first, until - first))
        first = until

    def last(sub):
        return row(rows_y - 1) if sub == 0 else high(sub - 1)

    block(blocks - 1, carry, last)
    sent.append(send(chunks, blocks - 1, 1))
    for copy in sent:
        copy.wait()


def stage_kernel(fluid_ref, out_ref, sem):
    copy = pltpu.make_async_copy(fluid_ref, out_ref, sem)
    copy.start()
    copy.wait()


def staged(fluid):
    return pl.pallas_call(
        stage_kernel,
        out_shape=jax.ShapeDtypeStruct(fluid.shape, jnp.float32),
        in_specs=[pl.BlockSpec(memory_space=pl.ANY)],
        out_specs=pl.BlockSpec(memory_space=pltpu.VMEM),
        scratch_shapes=[pltpu.SemaphoreType.DMA],
        compiler_params=pltpu.CompilerParams(vmem_limit_bytes=int(51.5 * 1024 * 1024)),
        cost_estimate=pl.CostEstimate(flops=0, bytes_accessed=2_700_000, transcendentals=0),
        name="stage",
    )(fluid)


def sweep_y(fluid, inner, outer, blocks):
    nx, ny, nz = fluid.shape[1:]
    rows = nx * ny // blocks
    return pl.pallas_call(
        sweep_y_kernel,
        out_shape=jax.ShapeDtypeStruct((blocks, 5, rows, nz), jnp.float32),
        in_specs=[pl.BlockSpec(memory_space=pltpu.VMEM)] * 3,
        out_specs=pl.BlockSpec(memory_space=pl.ANY),
        scratch_shapes=[
            pltpu.VMEM((blocks, 5, rows, nz), jnp.float32),
            pltpu.SemaphoreType.DMA((5,)),
        ],
        compiler_params=pltpu.CompilerParams(vmem_limit_bytes=16 * 1024 * 1024),
        cost_estimate=pl.CostEstimate(
            flops=20_000_000, bytes_accessed=2_700_000, transcendentals=0
        ),
        name="sweep_y",
    )(fluid, inner, outer)


def outer_peaks(floor_ref, ids_ref, code_ref, own_ref, below_ref, above_ref, peak_ref):
    lane = lax.broadcasted_iota(jnp.int32, (8, LANES), 1)
    lower = lane < LANES // 2

    def ends(ref, k):
        first = ref[0, k]
        return [first, pltpu.roll(first, LANES // 2, 1), ref[1, k]]

    states = [[own_ref[j, k] for k in range(5)] for j in range(9)]
    for k in range(5):
        for j, (b, a) in enumerate(zip(ends(below_ref, k), ends(above_ref, k))):
            states[j][k] = jnp.where(lower, b, states[j][k])
            states[6 + j][k] = jnp.where(lower, states[6 + j][k], a)
    faces = [face_of(*states[j : j + 4]) for j in range(6)]
    edges = [edges_of(states[j + 2], faces[j], faces[j + 1]) for j in range(5)]
    fluxes = [flux_of(edges[j][1], edges[j + 1][0], 3) for j in range(4)]
    tables = [updated(states[j + 3], fluxes[j], fluxes[j + 1])[4] for j in range(3)]
    planes = lax.broadcasted_iota(jnp.int32, (8, LANES), 0)
    for j in range(floor_ref.shape[0]):
        ids = jnp.broadcast_to(ids_ref[j : j + 1, :], (8, LANES))
        code = jnp.broadcast_to(code_ref[j : j + 1, :], (8, LANES))
        value = jnp.zeros((8, LANES), jnp.float32)
        for n, table in enumerate(tables):
            picked = jnp.take_along_axis(table, ids, axis=1, mode="promise_in_bounds")
            value = jnp.where(code == planes + 8 * n, picked, value)
        raised = jnp.sum(value, axis=0, keepdims=True)
        peak_ref[j : j + 1, :] = jnp.maximum(floor_ref[j : j + 1, :], raised)


def sweep_z_kernel(lines_ref, floor_ref, ids_ref, code_ref, own_ref, below_ref, above_ref, band_ref,
                   out_ref, peaks_ref, mid_ref, face_ref, left_ref, right_ref, flux_ref, new_ref, peak_ref, out_sem, peak_sem):
    tiles, _, rows, _ = lines_ref.shape
    steps = rows // 8
    lane = lax.broadcasted_iota(jnp.int32, (8, LANES), 1)

    def cell(q, t):
        return [lines_ref[t % tiles, k, pl.ds(8 * q, 8), :] for k in range(5)]

    def get(ref, q, t):
        return [ref[q % 2, t % tiles, k] for k in range(5)]

    def put(ref, q, t, values):
        for k in range(5):
            ref[q % 2, t, k] = values[k]

    def halves(values):
        high = values.astype(jnp.bfloat16)
        return high, (values - high.astype(jnp.float32)).astype(jnp.bfloat16)

    def stage_mid(q):
        wide = lax.broadcasted_iota(jnp.int32, (8 * tiles, LANES), 1)
        rows_x, rows_b = [], []
        for k in range(5):
            here = jnp.concatenate([lines_ref[t, k, 8 * q : 8 * q + 8, :] for t in range(tiles)], axis=0)
            before = jnp.concatenate([here[-8:], here[:-8]], axis=0)
            following = jnp.concatenate([here[8:], here[:8]], axis=0)
            rows_x.append(here)
            rows_b.append(jnp.where(wide == LANES - 1, before, following))
        x_high, x_low = halves(jnp.concatenate(rows_x, axis=0))
        b_high, b_low = halves(jnp.concatenate(rows_b, axis=0))
        mid_ref[q % 2] = jnp.dot(
            jnp.concatenate([x_high, b_high, x_low, b_low], axis=1),
            band_ref[...],
            preferred_element_type=jnp.float32,
        )

    def stage_face(q, t):
        here = cell(q, t)
        found = []
        for k in range(5):
            part = pl.ds(8 * (k * tiles + t), 8)
            mid = (1.0 / 12.0) * mid_ref[q % 2, part, :LANES]
            after = mid_ref[q % 2, part, LANES:]
            found.append(
                jnp.minimum(jnp.maximum(mid, jnp.minimum(here[k], after)), jnp.maximum(here[k], after))
            )
        put(face_ref, q, t, found)

    def stage_edges(q, t):
        face = get(face_ref, q, t)
        left, right = edges_of(
            cell(q, t), lane_before(face, get(face_ref, q, t - 1), lane), face
        )
        put(left_ref, q, t, left)
        put(right_ref, q, t, right)

    def stage_flux(q, t):
        follow = lane_after(get(left_ref, q, t), get(left_ref, q, t + 1), lane)
        put(flux_ref, q, t, flux_of(get(right_ref, q, t), follow, 3))

    def stage_new(q, t):
        flux = get(flux_ref, q, t)
        new = updated(cell(q, t), lane_before(flux, get(flux_ref, q, t - 1), lane), flux)
        for k in range(5):
            for half in range(2):
                place = pl.ds(t * LANES, LANES)
                new_ref[k, 2 * q + half, :, place] = new[k][4 * half : 4 * half + 4]

    outer_peaks(floor_ref, ids_ref, code_ref, own_ref, below_ref, above_ref, peak_ref)
    sent = [pltpu.make_async_copy(peak_ref, peaks_ref, peak_sem)]
    stages = (stage_face, stage_edges, stage_flux, stage_new)
    stage_mid(0)
    for step in range(steps + 3):
        if step + 1 < steps:
            stage_mid(step + 1)
        for start in range(0, tiles, 4):
            for age, stage in enumerate(stages):
                q = step - age
                if 0 <= q < steps:
                    for t in range(start, start + 4):
                        stage(q, t)
        q = step - 3
        if q == 0:
            sent[0].start()
        if q >= 0:
            part = pl.ds(2 * q, 2)
            copy = pltpu.make_async_copy(new_ref.at[:, part], out_ref.at[:, part], out_sem.at[q])
            copy.start()
            sent.append(copy)
    for copy in sent:
        copy.wait()


def sweep_z(lines, floor, ids, code, own, below, above, band, nx):
    tiles, _, rows, _ = lines.shape
    shape = (5, nx, rows // nx, tiles * LANES)
    return pl.pallas_call(
        sweep_z_kernel,
        out_shape=(
            jax.ShapeDtypeStruct(shape, jnp.float32),
            jax.ShapeDtypeStruct(floor.shape, jnp.float32),
        ),
        in_specs=[pl.BlockSpec(memory_space=pltpu.VMEM)] * 8,
        out_specs=(pl.BlockSpec(memory_space=pl.ANY),) * 2,
        scratch_shapes=[pltpu.VMEM((2, 5 * 8 * tiles, 2 * LANES), jnp.float32)]
        + [pltpu.VMEM((2, tiles, 5, 8, LANES), jnp.float32)] * 4
        + [
            pltpu.VMEM(shape, jnp.float32),
            pltpu.VMEM(floor.shape, jnp.float32),
            pltpu.SemaphoreType.DMA((rows // 8,)),
            pltpu.SemaphoreType.DMA,
        ],
        compiler_params=pltpu.CompilerParams(vmem_limit_bytes=16 * 1024 * 1024),
        cost_estimate=pl.CostEstimate(
            flops=20_000_000, bytes_accessed=2_700_000, transcendentals=0
        ),
        name="sweep_z",
    )(lines, floor, ids, code, own, below, above, band)


def lines_of(states):
    def after(values):
        return [pltpu.roll(v, LANES - 1, 1) for v in values]

    def before(values):
        return [pltpu.roll(v, 1, 1) for v in values]

    nexts = [after(s) for s in states]
    faces = [face_of(before(s), s, n, after(n)) for s, n in zip(states, nexts)]
    edges = [edges_of(s, before(f), f) for s, f in zip(states, faces)]
    fluxes = [flux_of(right, after(left), 3) for left, right in edges]
    return [updated(s, before(f), f) for s, f in zip(states, fluxes)]


def band_matrix():
    source = lax.broadcasted_iota(jnp.int32, (4 * LANES, 2 * LANES), 0) % (2 * LANES)
    target = lax.broadcasted_iota(jnp.int32, (4 * LANES, 2 * LANES), 1)
    beside = source >= LANES
    cell = jnp.where(beside, source - LANES, source)
    cell = jnp.where(beside, jnp.where(cell == LANES - 1, -1, cell + LANES), cell)
    used = jnp.logical_not(beside) | (cell < LANES + 2)
    faces = target < LANES
    step = cell - jnp.where(faces, target, target - LANES)
    face = jnp.where((step == 0) | (step == 1), 7.0, jnp.where((step == -1) | (step == 2), -1.0, 0.0))
    value = jnp.where(faces, face, jnp.where(step == 1, 1.0, 0.0))
    return jnp.where(used, value, 0.0).astype(jnp.bfloat16)


def inner_kernel(owner_ref, count_ref, middle_ref, cell_ref, peak_ref, floor_ref, ids_ref, code_ref, own_ref,
                 up_ref, down_ref, band_ref, press_ref):
    blocks, _, rows, _ = middle_ref.shape
    lane = lax.broadcasted_iota(jnp.int32, (8, LANES), 1)
    lower = lane < LANES // 2

    def line(h, sub, k):
        return middle_ref[h, k, pl.ds(sub, 8, stride=4), :]

    def four(h, _):
        states = [[line(h, sub, k) for k in range(5)] for sub in range(4)]
        for sub, new in enumerate(lines_of(states)):
            press_ref[h, pl.ds(sub, 8, stride=4), :] = new[4]
        return 0

    lax.fori_loop(0, blocks, four, 0)
    ends = list(range(6)) + list(range(LANES - 6, LANES))
    group = 4
    for k in range(5):

        def gather(i, found):
            found = list(found)
            for at in range(4 * group):
                y = 4 * group * i + at
                moved = pltpu.roll(line(group * i + at // 4, at % 4, k), y, 1)
                for n, z in enumerate(ends):
                    found[n] = jnp.where(lane == (y + z) % LANES, moved, found[n])
            return tuple(found)

        zeros = (jnp.zeros((8, LANES), jnp.float32),) * len(ends)
        found = lax.fori_loop(0, blocks // group, gather, zeros)
        low = [pltpu.roll(found[z], (LANES - z) % LANES, 1) for z in range(6)]
        high = [pltpu.roll(found[6 + n], (LANES // 2 + 6 - n) % LANES, 1) for n in range(6)]
        own = high[:3] + [jnp.where(lower, l, h) for l, h in zip(low[:3], high[3:])] + low[3:]
        for j in range(9):
            own_ref[j, k] = own[j]
        turned = [pltpu.roll(v, LANES // 2, 1) for v in (own[3], own[5])]
        up_ref[0, k] = jnp.where(lower, turned[0], own[4])
        down_ref[0, k] = jnp.where(lower, own[4], turned[0])
        up_ref[1, k] = turned[1]
        down_ref[1, k] = turned[1]
    band_ref[...] = band_matrix()
    row_ids = lax.broadcasted_iota(jnp.int32, (rows, LANES), 0)
    slot = lax.broadcasted_iota(jnp.int32, (1, LANES), 1)
    for j in range(blocks):
        owner = owner_ref[j]
        cells = cell_ref[j : j + 1, :]
        z = cells % LANES
        picked = jnp.take_along_axis(
            press_ref[owner], jnp.broadcast_to(z, (rows, LANES)), axis=1, mode="promise_in_bounds"
        )
        chosen = jnp.broadcast_to(cells // LANES, (rows, LANES)) == row_ids
        sampled = jnp.sum(jnp.where(chosen, picked, 0.0), axis=0, keepdims=True)
        upper = z >= LANES - 3
        outer = upper | (z < 3)
        live = slot < count_ref[j]
        peak = peak_ref[j : j + 1, :]
        raised = jnp.where(outer, peak, jnp.maximum(peak, sampled))
        floor_ref[j : j + 1, :] = jnp.where(live, raised, 0.0)
        ids_ref[j : j + 1, :] = 4 * owner + cells // LANES % 4 + jnp.where(upper, LANES // 2, 0)
        table = jnp.where(upper, z - (LANES - 3), z)
        code_ref[j : j + 1, :] = jnp.where(outer & live, 8 * table + cells // (4 * LANES), -1)


def inner_samples(owner, count, middle, cells, peaks):
    blocks, _, rows, _ = middle.shape
    return pl.pallas_call(
        inner_kernel,
        out_shape=(
            jax.ShapeDtypeStruct(cells.shape, jnp.float32),
            jax.ShapeDtypeStruct(cells.shape, jnp.int32),
            jax.ShapeDtypeStruct(cells.shape, jnp.int32),
            jax.ShapeDtypeStruct((9, 5, 8, LANES), jnp.float32),
            jax.ShapeDtypeStruct((2, 5, 8, LANES), jnp.float32),
            jax.ShapeDtypeStruct((2, 5, 8, LANES), jnp.float32),
            jax.ShapeDtypeStruct((4 * LANES, 2 * LANES), jnp.bfloat16),
        ),
        in_specs=[pl.BlockSpec(memory_space=pltpu.SMEM)] * 2
        + [pl.BlockSpec(memory_space=pltpu.VMEM)] * 3,
        out_specs=(pl.BlockSpec(memory_space=pltpu.VMEM),) * 7,
        scratch_shapes=[pltpu.VMEM((blocks, rows, LANES), jnp.float32)],
        compiler_params=pltpu.CompilerParams(vmem_limit_bytes=16 * 1024 * 1024),
        cost_estimate=pl.CostEstimate(
            flops=20_000_000, bytes_accessed=1_600_000, transcendentals=0
        ),
        name="inner_samples",
    )(owner, count, middle, cells, peaks)


def shifted(values, axis, step):
    count = lax.axis_size(axis)
    return lax.ppermute(values, axis, [(i, (i + step) % count) for i in range(count)])


def on_device(fluid_state, tracer_cell, tracer_owner, tracer_count, tracer_peak):
    nx, ny = fluid_state.shape[1:3]
    blocks = lax.axis_size("gz")
    head = jnp.transpose(fluid_state[:, :, :3], (2, 0, 1, 3))
    tail = jnp.transpose(fluid_state[:, :, ny - 3 :], (2, 0, 1, 3))
    count = lax.axis_size("gy")
    odd = lax.axis_index("gy") % 2 == 1
    inner = [(i, i ^ 1) for i in range(count)]
    outer = [((i + 1) % count, ((i ^ 1) + 1) % count) for i in range(count)]
    got_inner = lax.ppermute(jnp.where(odd, head, tail), "gy", inner)
    got_outer = lax.ppermute(jnp.where(odd, tail, head), "gy", outer)
    middle = sweep_y(staged(fluid_state), got_inner, got_outer, blocks)
    lines = lax.all_to_all(middle, "gz", split_axis=0, concat_axis=0, tiled=True)
    floor, ids, code, own, up, down, band = inner_samples(
        tracer_owner[0, 0], tracer_count[0, 0], middle, tracer_cell[0, 0], tracer_peak[0, 0]
    )
    above = shifted(down, "gz", -1)
    below = shifted(up, "gz", 1)
    new_state, new_peak = sweep_z(lines, floor, ids, code, own, below, above, band, nx)
    return (new_state, new_peak[None, None])


def solution(mesh):
    in_specs = (
        P(None, None, "gy", "gz"),
        P("gy", "gz", None, None),
        P("gy", "gz", None),
        P("gy", "gz", None),
        P("gy", "gz", None, None),
    )
    out_specs = (P(None, None, ("gy", "gz"), None), P("gy", "gz", None, None))
    return jax.shard_map(
        on_device, mesh=mesh, in_specs=in_specs, out_specs=out_specs, check_vma=False
    )
```

```python
import jax
import jax.numpy as jnp
from jax import lax
from jax.experimental import pallas as pl
from jax.experimental.pallas import tpu as pltpu
from jax.sharding import PartitionSpec as P

GAMMA = 1.4
RATIO = 0.06
LANES = 128


def median_of(first, second, third):
    return jnp.maximum(jnp.minimum(first, second), jnp.minimum(jnp.maximum(first, second), third))


def face_of(before, left, right, after):
    out = []
    for b, l, r, a in zip(before, left, right, after):
        mid = (7.0 / 12.0) * (l + r) - (1.0 / 12.0) * (b + a)
        out.append(jnp.minimum(jnp.maximum(mid, jnp.minimum(l, r)), jnp.maximum(l, r)))
    return out


def edges_of(centre, face_left, face_right):
    left, right = [], []
    for a, fl, fr in zip(centre, face_left, face_right):
        triple = 3.0 * a
        left.append(median_of(a, fl, triple - 2.0 * fr))
        right.append(median_of(a, fr, triple - 2.0 * fl))
    return left, right


def inverse(value):
    return pl.reciprocal(value, approx=True)


def sound(rho, p):
    heat = GAMMA * p
    return heat * lax.rsqrt(jnp.maximum(heat * rho, 1e-30))


def flux_of(left, right, normal):
    rho_l, p_l, u_l = left[0], left[4], left[normal]
    rho_r, p_r, u_r = right[0], right[4], right[normal]
    c_l = sound(rho_l, p_l)
    c_r = sound(rho_r, p_r)
    slow = jnp.minimum(jnp.minimum(u_l - c_l, u_r - c_r), 0.0)
    fast = jnp.maximum(jnp.maximum(u_l + c_l, u_r + c_r), 0.0)
    scale = RATIO * inverse(fast - slow)
    a_l = fast * scale
    a_r = slow * scale
    w_l = a_l * (u_l - slow)
    w_r = a_r * (u_r - fast)
    q_l = rho_l * w_l
    q_r = rho_r * w_r
    flux = [q_l - q_r] + [q_l * left[k] - q_r * right[k] for k in (1, 2, 3)]
    push_l = a_l * p_l
    push_r = a_r * p_r
    flux[normal] = flux[normal] + (push_l - push_r)
    square_l = left[1] * left[1] + left[2] * left[2] + left[3] * left[3]
    square_r = right[1] * right[1] + right[2] * right[2] + right[3] * right[3]
    flux.append(
        0.2 * (q_l * square_l - q_r * square_r)
        + 0.4 * (push_l * u_l - push_r * u_r)
        + (p_l * w_l - p_r * w_r)
    )
    return flux


def updated(state, flux_left, flux_right):
    rho, vx, vy, vz, p = state
    change = [r - l for l, r in zip(flux_left, flux_right)]
    mom = [rho * v for v in (vx, vy, vz)]
    twice = mom[0] * vx + mom[1] * vy + mom[2] * vz
    rho_new = rho - change[0]
    mom_new = [m - d for m, d in zip(mom, change[1:4])]
    inv = inverse(rho_new)
    vel = [m * inv for m in mom_new]
    twice_new = mom_new[0] * vel[0] + mom_new[1] * vel[1] + mom_new[2] * vel[2]
    return [rho_new] + vel + [p - change[4] + 0.2 * (twice - twice_new)]


def lane_after(here, following, lane):
    return [
        pltpu.roll(jnp.where(lane == 0, f, h), LANES - 1, 1) for h, f in zip(here, following)
    ]


def lane_before(here, previous, lane):
    return [
        pltpu.roll(jnp.where(lane == LANES - 1, p, h), 1, 1) for h, p in zip(here, previous)
    ]


def sweep_y_kernel(fluid_ref, inner_ref, outer_ref, middle_ref, new_ref, out_sem):
    nx, rows_y = fluid_ref.shape[1:3]
    blocks = middle_ref.shape[0]
    chunks = 4
    odd = lax.axis_index("gy") % 2 == 1
    flat_ref = fluid_ref.reshape(5, nx * rows_y, LANES)

    def row(y):
        return [flat_ref[k, pl.ds(y, nx, stride=rows_y), :] for k in range(5)]

    def low(i):
        return [jnp.where(odd, inner_ref[i, k], outer_ref[i, k]) for k in range(5)]

    def high(i):
        return [jnp.where(odd, outer_ref[i, k], inner_ref[i, k]) for k in range(5)]

    def block(h, carry, load):
        flux, right, face, c0, c1, c2 = carry
        for sub in range(4):
            c3 = load(sub)
            face_next = face_of(c0, c1, c2, c3)
            left_next, right_next = edges_of(c1, face, face_next)
            flux_next = flux_of(right, left_next, 2)
            new = updated(c0, flux, flux_next)
            for k in range(5):
                new_ref[h, k, pl.ds(sub, 8, stride=4), :] = new[k]
            flux, right, face, c0, c1, c2 = flux_next, right_next, face_next, c1, c2, c3
        return flux, right, face, c0, c1, c2

    def step(h, carry):
        return block(h, carry, lambda sub: row(4 * h + sub + 3))

    def send(i, first, count):
        part = pl.ds(first, count)
        copy = pltpu.make_async_copy(new_ref.at[part], middle_ref.at[part], out_sem.at[i])
        copy.start()
        return copy

    m3, m2, m1 = low(0), low(1), low(2)
    c0, c1, c2 = row(0), row(1), row(2)
    face_a = face_of(m3, m2, m1, c0)
    face_b = face_of(m2, m1, c0, c1)
    face_c = face_of(m1, c0, c1, c2)
    _, right_a = edges_of(m1, face_a, face_b)
    left_b, right_b = edges_of(c0, face_b, face_c)
    carry = (flux_of(right_a, left_b, 2), right_b, face_c, c0, c1, c2)
    first = 0
    sent = []
    for c in range(chunks):
        until = (c + 1) * blocks // chunks - 1
        carry = lax.fori_loop(first, until, step, carry, unroll=True)
        sent.append(send(c, first, until - first))
        first = until

    def last(sub):
        return row(rows_y - 1) if sub == 0 else high(sub - 1)

    block(blocks - 1, carry, last)
    sent.append(send(chunks, blocks - 1, 1))
    for copy in sent:
        copy.wait()


def stage_kernel(fluid_ref, out_ref, sem):
    copy = pltpu.make_async_copy(fluid_ref, out_ref, sem)
    copy.start()
    copy.wait()


def staged(fluid):
    return pl.pallas_call(
        stage_kernel,
        out_shape=jax.ShapeDtypeStruct(fluid.shape, jnp.float32),
        in_specs=[pl.BlockSpec(memory_space=pl.ANY)],
        out_specs=pl.BlockSpec(memory_space=pltpu.VMEM),
        scratch_shapes=[pltpu.SemaphoreType.DMA],
        compiler_params=pltpu.CompilerParams(vmem_limit_bytes=int(51.5 * 1024 * 1024)),
        cost_estimate=pl.CostEstimate(flops=0, bytes_accessed=2_700_000, transcendentals=0),
        name="stage",
    )(fluid)


def sweep_y(fluid, inner, outer, blocks):
    nx, ny, nz = fluid.shape[1:]
    rows = nx * ny // blocks
    return pl.pallas_call(
        sweep_y_kernel,
        out_shape=jax.ShapeDtypeStruct((blocks, 5, rows, nz), jnp.float32),
        in_specs=[pl.BlockSpec(memory_space=pltpu.VMEM)] * 3,
        out_specs=pl.BlockSpec(memory_space=pl.ANY),
        scratch_shapes=[
            pltpu.VMEM((blocks, 5, rows, nz), jnp.float32),
            pltpu.SemaphoreType.DMA((5,)),
        ],
        compiler_params=pltpu.CompilerParams(vmem_limit_bytes=16 * 1024 * 1024),
        cost_estimate=pl.CostEstimate(
            flops=20_000_000, bytes_accessed=2_700_000, transcendentals=0
        ),
        name="sweep_y",
    )(fluid, inner, outer)


def outer_peaks(floor_ref, ids_ref, code_ref, own_ref, below_ref, above_ref, peak_ref):
    lane = lax.broadcasted_iota(jnp.int32, (8, LANES), 1)
    lower = lane < LANES // 2

    def ends(ref, k):
        first, third = ref[k], ref[5 + k // 2]
        if k % 2 == 1:
            third = pltpu.roll(third, LANES // 2, 1)
        return [first, pltpu.roll(first, LANES // 2, 1), third]

    states = [[own_ref[j, k] for k in range(5)] for j in range(9)]
    for k in range(5):
        for j, (b, a) in enumerate(zip(ends(below_ref, k), ends(above_ref, k))):
            states[j][k] = jnp.where(lower, b, states[j][k])
            states[6 + j][k] = jnp.where(lower, states[6 + j][k], a)
    faces = [face_of(*states[j : j + 4]) for j in range(6)]
    edges = [edges_of(states[j + 2], faces[j], faces[j + 1]) for j in range(5)]
    fluxes = [flux_of(edges[j][1], edges[j + 1][0], 3) for j in range(4)]
    tables = [updated(states[j + 3], fluxes[j], fluxes[j + 1])[4] for j in range(3)]
    planes = lax.broadcasted_iota(jnp.int32, (8, LANES), 0)
    for j in range(floor_ref.shape[0]):
        ids = jnp.broadcast_to(ids_ref[j : j + 1, :], (8, LANES))
        code = jnp.broadcast_to(code_ref[j : j + 1, :], (8, LANES))
        value = jnp.zeros((8, LANES), jnp.float32)
        for n, table in enumerate(tables):
            picked = jnp.take_along_axis(table, ids, axis=1, mode="promise_in_bounds")
            value = jnp.where(code == planes + 8 * n, picked, value)
        raised = jnp.sum(value, axis=0, keepdims=True)
        peak_ref[j : j + 1, :] = jnp.maximum(floor_ref[j : j + 1, :], raised)


def sweep_z_kernel(lines_ref, floor_ref, ids_ref, code_ref, own_ref, below_ref, above_ref, band_ref,
                   out_ref, peaks_ref, mid_ref, face_ref, left_ref, right_ref, flux_ref, new_ref, peak_ref, out_sem, peak_sem):
    tiles, _, rows, _ = lines_ref.shape
    steps = rows // 8
    lane = lax.broadcasted_iota(jnp.int32, (8, LANES), 1)

    def cell(q, t):
        return [lines_ref[t % tiles, k, pl.ds(8 * q, 8), :] for k in range(5)]

    def get(ref, q, t):
        return [ref[q % 2, t % tiles, k] for k in range(5)]

    def put(ref, q, t, values):
        for k in range(5):
            ref[q % 2, t, k] = values[k]

    def halves(values):
        high = values.astype(jnp.bfloat16)
        return high, (values - high.astype(jnp.float32)).astype(jnp.bfloat16)

    def stage_mid(q):
        wide = lax.broadcasted_iota(jnp.int32, (8 * tiles, LANES), 1)
        rows_x, rows_b = [], []
        for k in range(5):
            here = jnp.concatenate([lines_ref[t, k, 8 * q : 8 * q + 8, :] for t in range(tiles)], axis=0)
            before = jnp.concatenate([here[-8:], here[:-8]], axis=0)
            following = jnp.concatenate([here[8:], here[:8]], axis=0)
            rows_x.append(here)
            rows_b.append(jnp.where(wide == LANES - 1, before, following))
        x_high, x_low = halves(jnp.concatenate(rows_x, axis=0))
        b_high, b_low = halves(jnp.concatenate(rows_b, axis=0))
        mid_ref[q % 2] = jnp.dot(
            jnp.concatenate([x_high, b_high, x_low, b_low], axis=1),
            band_ref[...],
            preferred_element_type=jnp.float32,
        )

    def stage_face(q, t):
        here = cell(q, t)
        found = []
        for k in range(5):
            part = pl.ds(8 * (k * tiles + t), 8)
            mid = (1.0 / 12.0) * mid_ref[q % 2, part, :LANES]
            after = mid_ref[q % 2, part, LANES:]
            found.append(
                jnp.minimum(jnp.maximum(mid, jnp.minimum(here[k], after)), jnp.maximum(here[k], after))
            )
        put(face_ref, q, t, found)

    def stage_edges(q, t):
        face = get(face_ref, q, t)
        left, right = edges_of(
            cell(q, t), lane_before(face, get(face_ref, q, t - 1), lane), face
        )
        put(left_ref, q, t, left)
        put(right_ref, q, t, right)

    def stage_flux(q, t):
        follow = lane_after(get(left_ref, q, t), get(left_ref, q, t + 1), lane)
        put(flux_ref, q, t, flux_of(get(right_ref, q, t), follow, 3))

    def stage_new(q, t):
        flux = get(flux_ref, q, t)
        new = updated(cell(q, t), lane_before(flux, get(flux_ref, q, t - 1), lane), flux)
        for k in range(5):
            for half in range(2):
                place = pl.ds(t * LANES, LANES)
                new_ref[k, 2 * q + half, :, place] = new[k][4 * half : 4 * half + 4]

    outer_peaks(floor_ref, ids_ref, code_ref, own_ref, below_ref, above_ref, peak_ref)
    sent = [pltpu.make_async_copy(peak_ref, peaks_ref, peak_sem)]
    stages = (stage_face, stage_edges, stage_flux, stage_new)
    stage_mid(0)
    for step in range(steps + 3):
        if step + 1 < steps:
            stage_mid(step + 1)
        for start in range(0, tiles, 4):
            for age, stage in enumerate(stages):
                q = step - age
                if 0 <= q < steps:
                    for t in range(start, start + 4):
                        stage(q, t)
        q = step - 3
        if q == 0:
            sent[0].start()
        if q >= 0:
            part = pl.ds(2 * q, 2)
            copy = pltpu.make_async_copy(new_ref.at[:, part], out_ref.at[:, part], out_sem.at[q])
            copy.start()
            sent.append(copy)
    for copy in sent:
        copy.wait()


def sweep_z(lines, floor, ids, code, own, below, above, band, nx):
    tiles, _, rows, _ = lines.shape
    shape = (5, nx, rows // nx, tiles * LANES)
    return pl.pallas_call(
        sweep_z_kernel,
        out_shape=(
            jax.ShapeDtypeStruct(shape, jnp.float32),
            jax.ShapeDtypeStruct(floor.shape, jnp.float32),
        ),
        in_specs=[pl.BlockSpec(memory_space=pltpu.VMEM)] * 8,
        out_specs=(pl.BlockSpec(memory_space=pl.ANY),) * 2,
        scratch_shapes=[pltpu.VMEM((2, 5 * 8 * tiles, 2 * LANES), jnp.float32)]
        + [pltpu.VMEM((2, tiles, 5, 8, LANES), jnp.float32)] * 4
        + [
            pltpu.VMEM(shape, jnp.float32),
            pltpu.VMEM(floor.shape, jnp.float32),
            pltpu.SemaphoreType.DMA((rows // 8,)),
            pltpu.SemaphoreType.DMA,
        ],
        compiler_params=pltpu.CompilerParams(vmem_limit_bytes=16 * 1024 * 1024),
        cost_estimate=pl.CostEstimate(
            flops=20_000_000, bytes_accessed=2_700_000, transcendentals=0
        ),
        name="sweep_z",
    )(lines, floor, ids, code, own, below, above, band)


def lines_of(states):
    def after(values):
        return [pltpu.roll(v, LANES - 1, 1) for v in values]

    def before(values):
        return [pltpu.roll(v, 1, 1) for v in values]

    nexts = [after(s) for s in states]
    faces = [face_of(before(s), s, n, after(n)) for s, n in zip(states, nexts)]
    edges = [edges_of(s, before(f), f) for s, f in zip(states, faces)]
    fluxes = [flux_of(right, after(left), 3) for left, right in edges]
    return [updated(s, before(f), f) for s, f in zip(states, fluxes)]


def band_matrix():
    source = lax.broadcasted_iota(jnp.int32, (4 * LANES, 2 * LANES), 0) % (2 * LANES)
    target = lax.broadcasted_iota(jnp.int32, (4 * LANES, 2 * LANES), 1)
    beside = source >= LANES
    cell = jnp.where(beside, source - LANES, source)
    cell = jnp.where(beside, jnp.where(cell == LANES - 1, -1, cell + LANES), cell)
    used = jnp.logical_not(beside) | (cell < LANES + 2)
    faces = target < LANES
    step = cell - jnp.where(faces, target, target - LANES)
    face = jnp.where((step == 0) | (step == 1), 7.0, jnp.where((step == -1) | (step == 2), -1.0, 0.0))
    value = jnp.where(faces, face, jnp.where(step == 1, 1.0, 0.0))
    return jnp.where(used, value, 0.0).astype(jnp.bfloat16)


def inner_kernel(owner_ref, count_ref, middle_ref, cell_ref, peak_ref, floor_ref, ids_ref, code_ref, own_ref,
                 up_ref, down_ref, band_ref, press_ref):
    blocks, _, rows, _ = middle_ref.shape
    lane = lax.broadcasted_iota(jnp.int32, (8, LANES), 1)
    lower = lane < LANES // 2

    def line(h, sub, k):
        return middle_ref[h, k, pl.ds(sub, 8, stride=4), :]

    def four(h, _):
        states = [[line(h, sub, k) for k in range(5)] for sub in range(4)]
        for sub, new in enumerate(lines_of(states)):
            press_ref[h, pl.ds(sub, 8, stride=4), :] = new[4]
        return 0

    lax.fori_loop(0, blocks, four, 0)
    ends = list(range(6)) + list(range(LANES - 6, LANES))
    group = 4
    for k in range(5):

        def gather(i, found):
            found = list(found)
            for at in range(4 * group):
                y = 4 * group * i + at
                moved = pltpu.roll(line(group * i + at // 4, at % 4, k), y, 1)
                for n, z in enumerate(ends):
                    found[n] = jnp.where(lane == (y + z) % LANES, moved, found[n])
            return tuple(found)

        zeros = (jnp.zeros((8, LANES), jnp.float32),) * len(ends)
        found = lax.fori_loop(0, blocks // group, gather, zeros)
        low = [pltpu.roll(found[z], (LANES - z) % LANES, 1) for z in range(6)]
        high = [pltpu.roll(found[6 + n], (LANES // 2 + 6 - n) % LANES, 1) for n in range(6)]
        own = high[:3] + [jnp.where(lower, l, h) for l, h in zip(low[:3], high[3:])] + low[3:]
        for j in range(9):
            own_ref[j, k] = own[j]
        turned = [pltpu.roll(v, LANES // 2, 1) for v in (own[3], own[5])]
        up_ref[k] = jnp.where(lower, turned[0], own[4])
        down_ref[k] = jnp.where(lower, own[4], turned[0])
        if k % 2 == 0:
            even = turned[1]
            up_ref[5 + k // 2] = even
            down_ref[5 + k // 2] = even
        else:
            up_ref[5 + k // 2] = jnp.where(lower, even, own[5])
            down_ref[5 + k // 2] = jnp.where(lower, own[5], even)
    band_ref[...] = band_matrix()
    row_ids = lax.broadcasted_iota(jnp.int32, (rows, LANES), 0)
    slot = lax.broadcasted_iota(jnp.int32, (1, LANES), 1)
    for j in range(blocks):
        owner = owner_ref[j]
        cells = cell_ref[j : j + 1, :]
        z = cells % LANES
        picked = jnp.take_along_axis(
            press_ref[owner], jnp.broadcast_to(z, (rows, LANES)), axis=1, mode="promise_in_bounds"
        )
        chosen = jnp.broadcast_to(cells // LANES, (rows, LANES)) == row_ids
        sampled = jnp.sum(jnp.where(chosen, picked, 0.0), axis=0, keepdims=True)
        upper = z >= LANES - 3
        outer = upper | (z < 3)
        live = slot < count_ref[j]
        peak = peak_ref[j : j + 1, :]
        raised = jnp.where(outer, peak, jnp.maximum(peak, sampled))
        floor_ref[j : j + 1, :] = jnp.where(live, raised, 0.0)
        ids_ref[j : j + 1, :] = 4 * owner + cells // LANES % 4 + jnp.where(upper, LANES // 2, 0)
        table = jnp.where(upper, z - (LANES - 3), z)
        code_ref[j : j + 1, :] = jnp.where(outer & live, 8 * table + cells // (4 * LANES), -1)


def inner_samples(owner, count, middle, cells, peaks):
    blocks, _, rows, _ = middle.shape
    return pl.pallas_call(
        inner_kernel,
        out_shape=(
            jax.ShapeDtypeStruct(cells.shape, jnp.float32),
            jax.ShapeDtypeStruct(cells.shape, jnp.int32),
            jax.ShapeDtypeStruct(cells.shape, jnp.int32),
            jax.ShapeDtypeStruct((9, 5, 8, LANES), jnp.float32),
            jax.ShapeDtypeStruct((8, 8, LANES), jnp.float32),
            jax.ShapeDtypeStruct((8, 8, LANES), jnp.float32),
            jax.ShapeDtypeStruct((4 * LANES, 2 * LANES), jnp.bfloat16),
        ),
        in_specs=[pl.BlockSpec(memory_space=pltpu.SMEM)] * 2
        + [pl.BlockSpec(memory_space=pltpu.VMEM)] * 3,
        out_specs=(pl.BlockSpec(memory_space=pltpu.VMEM),) * 7,
        scratch_shapes=[pltpu.VMEM((blocks, rows, LANES), jnp.float32)],
        compiler_params=pltpu.CompilerParams(vmem_limit_bytes=16 * 1024 * 1024),
        cost_estimate=pl.CostEstimate(
            flops=20_000_000, bytes_accessed=1_600_000, transcendentals=0
        ),
        name="inner_samples",
    )(owner, count, middle, cells, peaks)


def shifted(values, axis, step):
    count = lax.axis_size(axis)
    return lax.ppermute(values, axis, [(i, (i + step) % count) for i in range(count)])


def on_device(fluid_state, tracer_cell, tracer_owner, tracer_count, tracer_peak):
    nx, ny = fluid_state.shape[1:3]
    blocks = lax.axis_size("gz")
    head = jnp.transpose(fluid_state[:, :, :3], (2, 0, 1, 3))
    tail = jnp.transpose(fluid_state[:, :, ny - 3 :], (2, 0, 1, 3))
    count = lax.axis_size("gy")
    odd = lax.axis_index("gy") % 2 == 1
    inner = [(i, i ^ 1) for i in range(count)]
    outer = [((i + 1) % count, ((i ^ 1) + 1) % count) for i in range(count)]
    got_inner = lax.ppermute(jnp.where(odd, head, tail), "gy", inner)
    got_outer = lax.ppermute(jnp.where(odd, tail, head), "gy", outer)
    middle = sweep_y(staged(fluid_state), got_inner, got_outer, blocks)
    lines = lax.all_to_all(middle, "gz", split_axis=0, concat_axis=0, tiled=True)
    floor, ids, code, own, up, down, band = inner_samples(
        tracer_owner[0, 0], tracer_count[0, 0], middle, tracer_cell[0, 0], tracer_peak[0, 0]
    )
    above = shifted(down, "gz", -1)
    below = shifted(up, "gz", 1)
    new_state, new_peak = sweep_z(lines, floor, ids, code, own, below, above, band, nx)
    return (new_state, new_peak[None, None])


def solution(mesh):
    in_specs = (
        P(None, None, "gy", "gz"),
        P("gy", "gz", None, None),
        P("gy", "gz", None),
        P("gy", "gz", None),
        P("gy", "gz", None, None),
    )
    out_specs = (P(None, None, ("gy", "gz"), None), P("gy", "gz", None, None))
    return jax.shard_map(
        on_device, mesh=mesh, in_specs=in_specs, out_specs=out_specs, check_vma=False
    )
```
